128 devices in a mesh: dp: 32 (over y, x_hi, z), outer: 4 (over x_lo, core).
Axes of the slice: x: 4 (x_hi: 2, x_lo: 2; x = x_hi * 2 + x_lo), y: 4, z: 4, core: 2. Of those that a mesh axis runs over, the one named last changes fastest.
Arguments:
- gradients: bfloat16 [128, 1048576], P(('dp', 'outer')), may hold values from -1 to 0.9921875, as said below
- dither: int32 [128, 1048576], P(('dp', 'outer')), may hold values from 0 to 63
- sign_words: int32 [32768], replicated, may hold values from -2147483648 to 2147483646
- level_values: int32 [16], replicated, may hold values from -32 to 32, as said below
- level_points: float32 [16], replicated, may hold values from -1 to 1, as said below
- params: float32 [1048576], replicated, may hold values from -0.3 to 0.3
- first_moment: float32 [1048576], replicated, may hold values from -0.03 to 0.03
- second_moment: float32 [1048576], replicated, may hold values from 2e-05 to 0.01
Outputs:
- new_params: float32 [1048576], replicated
- new_first: float32 [1048576], replicated
- new_second: float32 [1048576], replicated
- update: float32 [1048576], replicated
The draws below stay inside these ranges and needn't reach their ends.
Inputs may be any that keep to these rules, and one draw needn't show every extreme that they name: `gradients`: every entry is a whole multiple of 1/128. Strictly increasing and antisymmetric (level_values[15 - i] = -level_values[i]); the largest is exactly 32. Strictly increasing and antisymmetric (level_points[15 - i] = -level_points[i]); the largest is exactly 1.
All inputs are finite; a program needn't handle non-finite values.
Results may differ from the reference program's by a relative error of at most 0.0003.
Values sent between devices are 32-bit elements; how exact they have to be, the bound alone decides.
A program may use at most 128 MiB of HBM per device.

```python
import math
import jax
import jax.numpy as jnp
from jax import lax

HB = 256
BLOCKS = 4096
PARAMS = 1048576
RANKS = 128


def draw_gradients(key, part):
    key = jax.random.fold_in(key, 11)
    level_key = jax.random.fold_in(key, 0)
    steps_drawn = jax.random.randint(level_key, (RANKS, BLOCKS, HB), -128, 128)
    return (steps_drawn.astype(jnp.float32) / 128.0).reshape(RANKS, PARAMS).astype(jnp.bfloat16)


def level_grid(key):
    grid_key = jax.random.fold_in(key, 23)
    shuffled = jax.random.permutation(grid_key, 31)[:7] + 1
    inside = jnp.sort(shuffled).astype(jnp.int32)
    positive = jnp.concatenate([inside, jnp.array([32], jnp.int32)])
    return jnp.concatenate([-positive[::-1], positive])


def draw_level_values(key, part):
    return level_grid(key)


def draw_level_points(key, part):
    grid = level_grid(key)
    key = jax.random.fold_in(key, 37)
    positive = grid[8:].astype(jnp.float32)
    below = jnp.concatenate([2.0 * positive[:1], positive[1:] - positive[:-1]])
    above = positive[1:] - positive[:-1]
    nearest = jnp.minimum(below[:7], above)
    jitter = jax.random.uniform(key, (7,), jnp.float32, -0.4, 0.4)
    inside = (positive[:7] + jitter * nearest) / 32.0
    points = jnp.concatenate([inside, jnp.ones((1,), jnp.float32)])
    return jnp.concatenate([-points[::-1], points])


def plant(values, key, low, largest):
    longest = values.shape.index(max(values.shape))
    spots = []
    for shift in (0, 1):
        where = [jax.random.randint(jax.random.fold_in(key, axis), (), 0, length) for axis, length in enumerate(values.shape)]
        where[longest] = (where[longest] + shift) % values.shape[longest]
        spots.append(tuple(where))
    return values.at[spots[0]].set(low).at[spots[1]].set(largest)


def bell_draw(rng, shape, deviation, limit, kind=jnp.bfloat16):
    return jnp.clip(deviation * jax.random.normal(rng, shape, jnp.float32), -limit, limit).astype(kind)


def setup_inputs(seed: int = 0) -> dict:
    streams_of = jax.random.split(jax.random.key(seed), 9)
    gradients = draw_gradients(jax.random.fold_in(streams_of[8], 71), 0)
    dither = plant(jax.random.randint(streams_of[1], (RANKS, PARAMS), 0, 64), jax.random.fold_in(streams_of[1], 1), 0, 63).astype(jnp.int32)
    sign_words = plant(jax.random.randint(streams_of[2], (PARAMS // 32,), -2147483648, 2147483647), jax.random.fold_in(streams_of[2], 1), -2147483648, 2147483646).astype(jnp.int32)
    level_values = draw_level_values(jax.random.fold_in(streams_of[8], 71), 0)
    level_points = draw_level_points(jax.random.fold_in(streams_of[8], 71), 0)
    params = bell_draw(streams_of[5], (PARAMS,), 0.05, 0.3, jnp.float32)
    first_moment = bell_draw(streams_of[6], (PARAMS,), 0.005, 0.03, jnp.float32)
    second_moment = jnp.clip(jnp.exp(jax.random.uniform(streams_of[7], (PARAMS,), jnp.float32, math.log(1.9999999494757503e-05), math.log(0.01))), 1.9999999494757503e-05, 0.01)
    return {"gradients": gradients, "dither": dither, "sign_words": sign_words, "level_values": level_values, "level_points": level_points, "params": params, "first_moment": first_moment, "second_moment": second_moment}


beta_first = 0.9
beta_second = 0.95
bias_first = 1.0 - 0.9 ** 50
bias_second = 1.0 - 0.95 ** 50
epsilon = 1e-08
step_rate = 0.01

def hadamard(length):
    indices = jnp.arange(length, dtype=jnp.int32)
    common = indices[:, None] & indices[None, :]
    parity = jnp.zeros((length, length), jnp.int32)
    for bit_pos in range(length.bit_length() - 1):
        parity = parity ^ common >> bit_pos & 1
    return 1 - 2 * parity

def sign_table(sign_words):
    bit_idx = jnp.arange(32, dtype=jnp.int32)
    sign_bits = sign_words[:, None] >> bit_idx[None, :] & 1
    return (1 - 2 * sign_bits).reshape(-1)

def rotate(grad_row, sign_vals, hadamard_bf):
    length = hadamard_bf.shape[0]
    scaled = (grad_row.astype(jnp.float32) * 128.0 * sign_vals.astype(jnp.float32)).astype(jnp.bfloat16)
    rotated = jnp.dot(scaled.reshape(-1, length), hadamard_bf, preferred_element_type=jnp.float32)
    return rotated.astype(jnp.int32)

def quantize(coeffs, peak_vals, level_values, level_points, dither):
    last_idx = level_values.shape[0] - 1
    target = coeffs * level_values[last_idx]
    peak_col = peak_vals[:, None]
    lower = jnp.zeros(target.shape, jnp.int32) + level_values[0]
    upper = jnp.zeros(target.shape, jnp.int32) + level_values[1]
    lower_point = jnp.zeros(target.shape, jnp.float32) + level_points[0]
    upper_point = jnp.zeros(target.shape, jnp.float32) + level_points[1]
    for level_idx in range(1, last_idx):
        passed = target >= peak_col * level_values[level_idx]
        lower = jnp.where(passed, level_values[level_idx], lower)
        upper = jnp.where(passed, level_values[level_idx + 1], upper)
        lower_point = jnp.where(passed, level_points[level_idx], lower_point)
        upper_point = jnp.where(passed, level_points[level_idx + 1], upper_point)
    rounds_up = 64 * (target - peak_col * lower) > dither * peak_col * (upper - lower)
    return jnp.where(rounds_up, upper_point, lower_point)

def decode_adam(totals, peak_vals, sign_vals, hadamard_mat, params, first_moment, second_moment, rank_count):
    length = totals.shape[1]
    restored = jnp.dot(totals.astype(jnp.float32), hadamard_mat.astype(jnp.float32), precision=lax.Precision.HIGHEST)
    factor = peak_vals.astype(jnp.float32) / float(128 * length * rank_count)
    mean_grad = (restored * factor[:, None]).reshape(-1) * sign_vals.astype(jnp.float32)
    new_first = beta_first * first_moment + (1.0 - beta_first) * mean_grad
    new_second = beta_second * second_moment + (1.0 - beta_second) * mean_grad * mean_grad
    update = new_first / bias_first / (jnp.sqrt(new_second / bias_second) + epsilon)
    new_params = params - step_rate * update
    return (new_params, new_first, new_second, update)

def reference(gradients, dither, sign_words, level_values, level_points, params, first_moment, second_moment):
    length = HB
    hadamard_mat = hadamard(length)
    hadamard_bf = hadamard_mat.astype(jnp.bfloat16)
    sign_vals = sign_table(sign_words)

    def peak_of(running, grad_row):
        coeffs = rotate(grad_row, sign_vals, hadamard_bf)
        return (jnp.maximum(running, lax.optimization_barrier(jnp.max(jnp.abs(coeffs), axis=1))), None)
    peak_vals, unused = lax.scan(peak_of, jnp.zeros((BLOCKS,), jnp.int32), gradients)

    def add_codes(running, inputs):
        grad_row, dither_row = inputs
        coeffs = rotate(grad_row, sign_vals, hadamard_bf)
        codes = quantize(coeffs, peak_vals, level_values, level_points, dither_row.reshape(-1, length))
        return (running + codes, None)
    totals, unused = lax.scan(add_codes, jnp.zeros((BLOCKS, length), jnp.float32), (gradients, dither))
    new_params, new_first, new_second, update = decode_adam(totals, peak_vals, sign_vals, hadamard_mat, params, first_moment, second_moment, RANKS)
    return (new_params, new_first, new_second, update)
```

```python
import jax
import jax.numpy as jnp
from jax import lax
from jax.experimental import pallas as pl
from jax.experimental.pallas import tpu as pltpu
from jax.sharding import PartitionSpec as P

MESH = pl.DeviceIdType.MESH
LANES = 128
UNIT = 8
ROWS = 8192
HALF_ROWS = ROWS // 2
CHUNK = 1024
RING = 4
SEGMENTS = ((0, 192), (192, 192), (384, 128))
ORDERS = (("x", "y", "z"), ("y", "z", "x"), ("z", "x", "y"))

beta_first = 0.9
beta_second = 0.95
bias_first = 1.0 - 0.9**50
bias_second = 1.0 - 0.95**50
epsilon = 1e-08
step_rate = 0.01


def rows_of(start, count):
    return pl.ds(pl.multiple_of(start * UNIT, UNIT), count * UNIT)


def take(table, idx):
    return jnp.take_along_axis(table, idx, axis=1, mode="promise_in_bounds")


def hadamard_128(length):
    common = lax.broadcasted_iota(jnp.int32, (length, length), 0) & lax.broadcasted_iota(
        jnp.int32, (length, length), 1
    )
    for shift in (4, 2, 1):
        common = common ^ (common >> shift)
    return jnp.where((common & 1) == 1, -128.0, 128.0).astype(jnp.float32)


class Place:
    def __init__(self):
        dp, outer = lax.axis_index("dp"), lax.axis_index("outer")
        self.at = {
            "y": lax.div(dp, 8),
            "x": lax.rem(lax.div(dp, 4), 2) * 2 + lax.div(outer, 2),
            "z": lax.rem(dp, 4),
            "core": lax.rem(outer, 2),
        }

    def near(self, axis, delta):
        at = dict(self.at)
        size = 2 if axis == "core" else RING
        at[axis] = lax.rem(at[axis] + (delta % size), size)
        dp = at["y"] * 8 + lax.div(at["x"], 2) * 4 + at["z"]
        return {"dp": dp, "outer": lax.rem(at["x"], 2) * 2 + at["core"]}


class Copies:
    def __init__(self, send, recv):
        self.send, self.recv, self.used, self.all = send, recv, 0, []

    def start(self, src, dst, to):
        copy = pltpu.make_async_remote_copy(
            src_ref=src,
            dst_ref=dst,
            send_sem=self.send.at[self.used],
            recv_sem=self.recv.at[self.used],
            device_id=to,
            device_id_type=MESH,
        )
        self.used += 1
        self.all.append(copy)
        copy.start()
        return copy

    def finish(self):
        for copy in self.all:
            copy.wait_send()


COPIES = 10 + 3 + 54 + 54 + 12


def layout():
    places, used = {}, 0
    for stage in range(3):
        for seg, (_, size) in enumerate(SEGMENTS):
            quarter = size // RING ** (stage + 1)
            low = quarter // 2
            for name, count in (("tl", low), ("th", quarter - low), ("fa", quarter), ("fb", quarter)):
                places[stage, seg, name] = (used, count)
                used += count
    return places, used


def add_into(dst, start, sources, count):
    step = 8 if count % 8 == 0 and count > 12 else count

    def body(i, carry):
        here = rows_of(start + i * step, step)
        value = dst[here, :]
        for ref, first in sources:
            value = value + ref[rows_of(first + i * step, step), :]
        dst[here, :] = value
        return carry

    if step == count:
        body(0, 0)
    else:
        lax.fori_loop(0, count // step, body, 0)


def reduce_kernel(
    grad_hbm, dither_hbm, words, level_values, level_points, out,
    grad_v, dither_v, signed, coef_even, coef_odd, codes, peaks, scaled, recip, peak_in,
    sibling_in, landing, owned, send_sems, recv_sems, grad_sems, dither_sem,
):
    here = Place()
    copies = Copies(send_sems, recv_sems)
    chunks = ROWS // CHUNK
    span = CHUNK * LANES
    loads = [
        pltpu.make_async_copy(
            grad_hbm.at[:, pl.ds(i * span, span)], grad_v.at[:, pl.ds(i * span, span)], grad_sems.at[i]
        )
        for i in range(chunks)
    ]
    for load in loads:
        load.start()
    dither_load = pltpu.make_async_copy(dither_hbm, dither_v, dither_sem)
    dither_load.start()

    barrier = pltpu.get_barrier_semaphore()
    partners = [here.near("core", 1)]
    for axis in ("x", "y", "z"):
        partners += [here.near(axis, delta) for delta in (1, 2, 3)]
    for partner in partners:
        pl.semaphore_signal(barrier, inc=1, device_id=partner, device_id_type=MESH)

    lane = lax.broadcasted_iota(jnp.int32, (UNIT, LANES), 1)
    sub = lax.broadcasted_iota(jnp.int32, (UNIT, LANES), 0)
    word_lane = sub * 4 + (lane >> 5)
    word_shift = 31 - (lane & 31)
    had = hadamard_128(2 * LANES)
    had_bf = had.astype(jnp.bfloat16)

    for i in range(chunks):
        loads[i].wait()

        def sign_rows(r, carry, i=i):
            word_row = i * (CHUNK // 32) + r
            wide = jnp.broadcast_to(words[pl.ds(word_row, 1), :], (UNIT, LANES))
            for k in range(4):
                word = take(wide, word_lane + 32 * k)
                first = pl.multiple_of(word_row * 4096 + k * 1024, 1024)
                grad = grad_v[:, pl.ds(first, 1024)].astype(jnp.float32).reshape(UNIT, LANES)
                signed[rows_of(r * 4 + k, 1), :] = jnp.where((word << word_shift) < 0, -grad, grad)
            return carry

        lax.fori_loop(0, CHUNK // 32, sign_rows, 0, unroll=4)
        even = signed[pl.ds(0, CHUNK // 2, stride=2), :]
        odd = signed[pl.ds(1, CHUNK // 2, stride=2), :]
        both = jnp.concatenate([even, odd], axis=1).astype(jnp.bfloat16)
        coeffs = jnp.dot(both, had_bf, preferred_element_type=jnp.float32)
        at = pl.ds(i * (CHUNK // 2), CHUNK // 2)
        coef_even[at, :] = coeffs[:, :LANES]
        coef_odd[at, :] = coeffs[:, LANES:]
        turned = lax.dot_general(
            had_bf, both, (((1,), (1,)), ((), ())), preferred_element_type=jnp.float32
        )
        top = jnp.max(jnp.abs(turned), axis=0, keepdims=True)
        for j in range(CHUNK // 256):
            peaks[pl.ds(i * (CHUNK // 256) + j, 1), :] = top[:, j * LANES : (j + 1) * LANES]

    pl.semaphore_wait(barrier, len(partners))
    used = 0
    for axis, deltas in (("core", (1,)), ("x", (1, 2, 3)), ("y", (1, 2, 3)), ("z", (1, 2, 3))):
        sent = []
        for delta in deltas:
            sent.append(copies.start(peaks, peak_in.at[used], here.near(axis, delta)))
            used += 1
        for copy in sent:
            copy.wait_recv()
            copy.wait_send()
        best = peaks[...]
        for slot in range(used - len(deltas), used):
            best = jnp.maximum(best, peak_in[slot])
        peaks[...] = best
    top = peaks[...]
    scaled[...] = top * (1.0 / 32.0)
    recip[...] = 32.0 / jnp.maximum(top, 1.0)

    cell = (lane & 63) - 32
    low = jnp.full((UNIT, LANES), level_values[0], jnp.int32)
    high = jnp.full((UNIT, LANES), level_values[1], jnp.int32)
    low_point = jnp.full((UNIT, LANES), level_points[0], jnp.float32)
    high_point = jnp.full((UNIT, LANES), level_points[1], jnp.float32)
    for j in range(1, 15):
        passed = cell >= level_values[j]
        low = jnp.where(passed, level_values[j], low)
        high = jnp.where(passed, level_values[j + 1], high)
        low_point = jnp.where(passed, level_points[j], low_point)
        high_point = jnp.where(passed, level_points[j + 1], high_point)
    gap_table = low.astype(jnp.float32) + (high - low).astype(jnp.float32) * (1.0 / 64.0)
    point_table = jnp.where(lane < 64, low_point, high_point)

    dither_load.wait()

    def quantize_rows(peak_row, add):
        scaled_row = jnp.broadcast_to(scaled[pl.ds(peak_row, 1), :], (UNIT, LANES))
        recip_row = jnp.broadcast_to(recip[pl.ds(peak_row, 1), :], (UNIT, LANES))
        for m in range(16):
            idx = sub + 8 * m
            peak32 = take(scaled_row, idx)
            ratio = take(recip_row, idx)
            peak_high = jnp.floor(peak32 * 0.125) * 8.0
            peak_low = peak32 - peak_high
            for parity, coef in ((0, coef_even), (1, coef_odd)):
                value = coef[rows_of(peak_row * 16 + m, 1), :]
                at = pl.ds(peak_row * 256 + (16 * m + parity), UNIT, stride=2)
                offset = dither_v[at, :].astype(jnp.float32)
                place = jnp.minimum((value * ratio + 32.0).astype(jnp.int32), 63)
                packed = take(gap_table, place)
                whole = jnp.floor(packed)
                bound = whole + offset * (packed - whole)
                up = (value - peak_high * bound) > peak_low * bound
                code = take(point_table, jnp.where(up, place + 64, place))
                if add:
                    near = pl.ds(lax.rem(peak_row, 16) * 256 + (16 * m + parity), UNIT, stride=2)
                    code = code + sibling_in[near, :]
                codes[at, :] = code

    core = here.at["core"]
    mine, theirs = core * 512, (1 - core) * 512
    sibling = here.near("core", 1)
    halves = []
    for first, size in SEGMENTS:

        def other(r, carry, first=first):
            quantize_rows((theirs + first) // 32 + r, False)
            return carry

        lax.fori_loop(0, size // 32, other, 0)
        halves.append(
            copies.start(codes.at[rows_of(theirs + first, size)], sibling_in.at[rows_of(first, size)], sibling)
        )

    places, _ = layout()

    def land(stage, seg, name, skip=0, count=None):
        first, size = places[stage, seg, name]
        return landing.at[rows_of(first + skip, size if count is None else count)]

    base = [mine + first for first, _ in SEGMENTS]
    bases = [[None] * 3 for _ in SEGMENTS]
    pending = {}

    def cut(stage, seg):
        quarter = SEGMENTS[seg][1] // RING ** (stage + 1)
        low_part = quarter // 2
        axis = ORDERS[seg][stage]
        p = here.at[axis]
        start = bases[seg][stage]
        part = [start + lax.rem(p + d, RING) * quarter for d in range(RING)]
        return quarter, low_part, part, here.near(axis, 1), here.near(axis, 3)

    def scatter_first(stage, seg):
        bases[seg][stage] = base[seg]
        quarter, low_part, part, right, left = cut(stage, seg)
        high_part = quarter - low_part
        pending[stage, seg] = [
            copies.start(codes.at[rows_of(part[2], low_part)], land(stage, seg, "tl"), right),
            copies.start(codes.at[rows_of(part[2] + low_part, high_part)], land(stage, seg, "th"), left),
            copies.start(
                codes.at[rows_of(part[1] + low_part, high_part)],
                land(stage, seg, "fa", low_part, high_part),
                right,
            ),
            copies.start(codes.at[rows_of(part[3], low_part)], land(stage, seg, "fb", 0, low_part), left),
        ]

    def scatter_second(stage, seg):
        quarter, low_part, part, right, left = cut(stage, seg)
        high_part = quarter - low_part
        waits = pending[stage, seg]
        waits[0].wait_recv()
        add_into(codes, part[1], [(landing, places[stage, seg, "tl"][0])], low_part)
        waits.append(
            copies.start(codes.at[rows_of(part[1], low_part)], land(stage, seg, "fa", 0, low_part), right)
        )
        waits[1].wait_recv()
        add_into(codes, part[3] + low_part, [(landing, places[stage, seg, "th"][0])], high_part)
        waits.append(
            copies.start(
                codes.at[rows_of(part[3] + low_part, high_part)],
                land(stage, seg, "fb", low_part, high_part),
                left,
            )
        )

    def scatter_last(stage, seg):
        quarter, _, part, _, _ = cut(stage, seg)
        for copy in pending[stage, seg][2:]:
            copy.wait_recv()
        add_into(
            codes,
            part[0],
            [(landing, places[stage, seg, "fa"][0]), (landing, places[stage, seg, "fb"][0])],
            quarter,
        )
        base[seg] = part[0]

    for seg, (first, size) in enumerate(SEGMENTS):
        halves[seg].wait_recv()

        def own(r, carry, first=first):
            quantize_rows((mine + first) // 32 + r, True)
            return carry

        lax.fori_loop(0, size // 32, own, 0)
        scatter_first(0, seg)

    for stage in range(3):
        for seg in range(3):
            scatter_second(stage, seg)
        for seg in range(3):
            scatter_last(stage, seg)
            if stage < 2:
                scatter_first(stage + 1, seg)

    units = [base[seg] + i for seg, (_, size) in enumerate(SEGMENTS) for i in range(size // 64)]
    for i, unit in enumerate(units):
        owned[pl.ds(i * UNIT, UNIT), :] = codes[rows_of(unit, 1), :]
    count = len(units) * UNIT // 2
    both = jnp.concatenate(
        [owned[pl.ds(0, count, stride=2), :], owned[pl.ds(1, count, stride=2), :]], axis=1
    )
    back = jnp.dot(both, had, precision=lax.Precision.HIGHEST, preferred_element_type=jnp.float32)
    owned[pl.ds(0, count, stride=2), :] = back[:, :LANES]
    owned[pl.ds(1, count, stride=2), :] = back[:, LANES:]
    for i, unit in enumerate(units):
        wide = jnp.broadcast_to(words[pl.ds(lax.div(unit, 4), 1), :], (UNIT, LANES))
        word = take(wide, word_lane + 32 * lax.rem(unit, 4))
        wide = jnp.broadcast_to(scaled[pl.ds(lax.div(unit, 32), 1), :], (UNIT, LANES))
        factor = take(wide, 4 * lax.rem(unit, 32) + (sub >> 1)) * (1.0 / 2.0**24)
        grad = owned[pl.ds(i * UNIT, UNIT), :] * factor
        out[rows_of(unit, 1), :] = jnp.where((word << word_shift) < 0, -grad, grad)

    def send(start, size, to):
        at = rows_of(start, size)
        return copies.start(out.at[at], out.at[at], to)

    last = []

    def gather_first(stage, seg):
        quarter, low_part, part, right, left = cut(stage, seg)
        high_part = quarter - low_part
        pending[stage, seg] = [
            send(part[0], low_part, right),
            send(part[0] + low_part, high_part, left),
            send(part[0] + low_part, high_part, right),
            send(part[0], low_part, left),
        ]
        if stage == 0:
            last.append(send(part[0], quarter, sibling))

    def gather_second(stage, seg):
        quarter, low_part, part, right, left = cut(stage, seg)
        high_part = quarter - low_part
        waits = pending[stage, seg]
        waits[0].wait_recv()
        waits.append(send(part[3], low_part, right))
        waits[1].wait_recv()
        waits.append(send(part[1] + low_part, high_part, left))
        waits[2].wait_recv()
        waits[3].wait_recv()
        if stage == 0:
            last.append(send(part[3], quarter, sibling))
            last.append(send(part[1], quarter, sibling))

    def gather_last(stage, seg):
        quarter, _, part, _, _ = cut(stage, seg)
        for copy in pending[stage, seg][4:]:
            copy.wait_recv()
        if stage == 0:
            last.append(send(part[2], quarter, sibling))

    for stage in (2, 1, 0):
        for seg in range(3):
            gather_first(stage, seg)
        for seg in range(3):
            gather_second(stage, seg)
        for seg in range(3):
            gather_last(stage, seg)
    for copy in last:
        copy.wait_recv()
    for copy in copies.all[10:]:
        copy.wait_send()


def mean_gradient(gradients, dither, sign_words, level_values, level_points):
    units = layout()[1]
    whole = pltpu.VMEM((ROWS, LANES), jnp.float32)
    half = pltpu.VMEM((HALF_ROWS, LANES), jnp.float32)
    peak = pltpu.VMEM((ROWS // 256, LANES), jnp.float32)
    anywhere = pl.BlockSpec(memory_space=pl.ANY)
    vmem = pl.BlockSpec(memory_space=pltpu.VMEM)
    smem = pl.BlockSpec(memory_space=pltpu.SMEM)
    return pl.pallas_call(
        reduce_kernel,
        out_shape=jax.ShapeDtypeStruct((ROWS, LANES), jnp.float32),
        in_specs=[anywhere, anywhere, vmem, smem, smem],
        out_specs=vmem,
        scratch_shapes=[
            pltpu.VMEM((1, ROWS * LANES), jnp.bfloat16),
            pltpu.VMEM((ROWS, LANES), jnp.int32),
            pltpu.VMEM((CHUNK, LANES), jnp.float32),
            half,
            half,
            whole,
            peak,
            peak,
            peak,
            pltpu.VMEM((10, ROWS // 256, LANES), jnp.float32),
            half,
            pltpu.VMEM((units * UNIT, LANES), jnp.float32),
            pltpu.VMEM((64, LANES), jnp.float32),
            pltpu.SemaphoreType.DMA((COPIES,)),
            pltpu.SemaphoreType.DMA((COPIES,)),
            pltpu.SemaphoreType.DMA((ROWS // CHUNK,)),
            pltpu.SemaphoreType.DMA,
        ],
        compiler_params=pltpu.CompilerParams(
            collective_id=0, has_side_effects=True, vmem_limit_bytes=44 * 2**20
        ),
        cost_estimate=pl.CostEstimate(flops=2**31, bytes_accessed=12 * 2**20, transcendentals=0),
    )(
        gradients,
        dither.reshape(ROWS, LANES),
        sign_words.reshape(-1, LANES),
        level_values,
        level_points,
    )


def body(
    gradients, dither, sign_words, level_values, level_points, params, first_moment, second_moment
):
    mean_grad = mean_gradient(gradients, dither, sign_words, level_values, level_points).reshape(-1)
    new_first = beta_first * first_moment + (1.0 - beta_first) * mean_grad
    new_second = beta_second * second_moment + (1.0 - beta_second) * mean_grad * mean_grad
    update = new_first / bias_first / (jnp.sqrt(new_second / bias_second) + epsilon)
    new_params = params - step_rate * update
    return (new_params, new_first, new_second, update)


def solution(mesh):
    placed = (P(("dp", "outer"), None), P(("dp", "outer"), None), P(), P(), P(), P(), P(), P())
    return jax.shard_map(
        body, mesh=mesh, in_specs=placed, out_specs=(P(), P(), P(), P()), check_vma=False
    )
```

```python
import jax
import jax.numpy as jnp
from jax import lax
from jax.experimental import pallas as pl
from jax.experimental.pallas import tpu as pltpu
from jax.sharding import PartitionSpec as P

MESH = pl.DeviceIdType.MESH
LANES = 128
UNIT = 8
ROWS = 8192
HALF_ROWS = ROWS // 2
CHUNK = 512
RING = 4
SEGMENTS = ((0, 192), (192, 192), (384, 128))
ORDERS = (("x", "y", "z"), ("y", "z", "x"), ("z", "x", "y"))
PLANE = tuple((i, j) for i in (2, 1, 3, 0) for j in (2, 1, 3, 0) if i + j)
GROUPS = (0, 1, 3, 2)
BATCH = 16
PEAK_ROWS = 2

beta_first = 0.9
beta_second = 0.95
bias_first = 1.0 - 0.9**50
bias_second = 1.0 - 0.95**50
epsilon = 1e-08
step_rate = 0.01


def rows_of(start, count):
    return pl.ds(pl.multiple_of(start * UNIT, UNIT), count * UNIT)


def take(table, idx):
    return jnp.take_along_axis(table, idx, axis=1, mode="promise_in_bounds")


def hadamard_128(length):
    common = lax.broadcasted_iota(jnp.int32, (length, length), 0) & lax.broadcasted_iota(
        jnp.int32, (length, length), 1
    )
    for shift in (4, 2, 1):
        common = common ^ (common >> shift)
    return jnp.where((common & 1) == 1, -128.0, 128.0).astype(jnp.float32)


class Place:
    def __init__(self):
        dp, outer = lax.axis_index("dp"), lax.axis_index("outer")
        self.at = {
            "y": lax.div(dp, 8),
            "x": lax.rem(lax.div(dp, 4), 2) * 2 + lax.div(outer, 2),
            "z": lax.rem(dp, 4),
            "core": lax.rem(outer, 2),
        }

    def near(self, *moves):
        at = dict(self.at)
        for axis, delta in moves:
            at[axis] = lax.rem(at[axis] + delta, 2 if axis == "core" else RING)
        dp = at["y"] * 8 + lax.div(at["x"], 2) * 4 + at["z"]
        return {"dp": dp, "outer": lax.rem(at["x"], 2) * 2 + at["core"]}


class Copies:
    def __init__(self, send, recv):
        self.send, self.recv, self.all = send, recv, []

    def start(self, src, dst, to):
        copy = pltpu.make_async_remote_copy(
            src_ref=src,
            dst_ref=dst,
            send_sem=self.send.at[len(self.all)],
            recv_sem=self.recv.at[len(self.all)],
            device_id=to,
            device_id_type=MESH,
        )
        self.all.append(copy)
        copy.start()
        return copy


PEAK_FIRST = tuple((("x", i), ("core", j)) for i in (2, 1, 3, 0) for j in (1, 0) if i + j)
PEAK_SECOND = tuple((("y", i), ("z", j)) for i, j in PLANE)
COPIES = 3 * (7 + 15 + 1 + 6 + 15 + 15 + 4 * 10)


def layout():
    places, used = {}, 0
    for seg, (_, size) in enumerate(SEGMENTS):
        quarter = size // RING
        low = quarter // 2
        for name, count in (
            ("tl", low),
            ("th", quarter - low),
            ("fa", quarter),
            ("fb", quarter),
            ("plane", quarter),
        ):
            places[seg, name] = (used, count)
            used += count
    return places, used


def add_into(dst, start, sources, count):
    step = 8 if count % 8 == 0 and count > 12 else count

    def body(i, carry):
        here = rows_of(start + i * step, step)
        value = dst[here, :]
        for ref, first in sources:
            value = value + ref[rows_of(first + i * step, step), :]
        dst[here, :] = value
        return carry

    if step == count:
        body(0, 0)
    else:
        lax.fori_loop(0, count // step, body, 0)


def reduce_kernel(
    grad_hbm, dither_hbm, words_hbm, values_hbm, points_hbm, out,
    grad_v, dither_v, words, level_values, level_points, signed, coef_even, coef_odd, codes,
    peak_a, peak_b, peak_c, first_in, second_in, high_all, low_all, ratio_all,
    sibling_in, landing, owned, send_sems, recv_sems, grad_sems, load_sems,
):
    here = Place()
    core = here.at["core"]
    copies = Copies(send_sems, recv_sems)
    peaks = (peak_a, peak_b, peak_c)
    sibling = here.near(("core", 1))
    mine, theirs = core * 512, (1 - core) * 512

    small_loads = [
        pltpu.make_async_copy(src, dst, load_sems.at[i])
        for i, (src, dst) in enumerate(
            ((words_hbm, words), (values_hbm, level_values), (points_hbm, level_points), (dither_hbm, dither_v))
        )
    ]
    span = CHUNK * LANES
    small_loads[0].start()
    steps = []
    for seg, (first, size) in enumerate(SEGMENTS):
        for half in (theirs, mine):
            steps += [(seg, half, (half + first) // 64 + i, i) for i in range(size // 64)]
    loads = []
    for i, (_, _, chunk, _) in enumerate(steps):
        at = pl.ds(pl.multiple_of(chunk * span, span), span)
        loads.append(pltpu.make_async_copy(grad_hbm.at[:, at], grad_v.at[:, at], grad_sems.at[i]))
        loads[-1].start()
    for load in small_loads[1:]:
        load.start()

    barrier = pltpu.get_barrier_semaphore()
    partners = [here.near(*moves) for moves in PEAK_FIRST + PEAK_SECOND]
    for a1, a2 in (("z", "x"), ("x", "y")):
        for i in (1, 2, 3):
            for j in (1, 2, 3):
                partners.append(here.near((a1, i), (a2, j)))
    for partner in partners:
        pl.semaphore_signal(barrier, inc=1, device_id=partner, device_id_type=MESH)

    lane = lax.broadcasted_iota(jnp.int32, (UNIT, LANES), 1)
    sub = lax.broadcasted_iota(jnp.int32, (UNIT, LANES), 0)
    word_lane = sub * 4 + (lane >> 5)
    word_shift = 31 - (lane & 31)
    had = hadamard_128(2 * LANES)
    had_bf = had.astype(jnp.bfloat16)
    for ref in peaks:
        ref[...] = jnp.zeros_like(ref)

    def rotate(step):
        seg, half, chunk, i = steps[step]
        loads[step].wait()

        def sign_rows(r, carry):
            word_row = chunk * (CHUNK // 32) + r
            wide = jnp.broadcast_to(words[pl.ds(word_row, 1), :], (UNIT, LANES))
            for k in range(4):
                word = take(wide, word_lane + 32 * k)
                first = pl.multiple_of(word_row * 4096 + k * 1024, 1024)
                grad = grad_v[:, pl.ds(first, 1024)].astype(jnp.float32).reshape(UNIT, LANES)
                signed[rows_of(r * 4 + k, 1), :] = jnp.where((word << word_shift) < 0, -grad, grad)
            return carry

        lax.fori_loop(0, CHUNK // 32, sign_rows, 0, unroll=4)
        even = signed[pl.ds(0, CHUNK // 2, stride=2), :]
        odd = signed[pl.ds(1, CHUNK // 2, stride=2), :]
        both = jnp.concatenate([even, odd], axis=1).astype(jnp.bfloat16)
        coeffs = jnp.dot(both, had_bf, preferred_element_type=jnp.float32)
        at = rows_of(chunk * 32, 32)
        coef_even[at, :] = coeffs[:, :LANES]
        coef_odd[at, :] = coeffs[:, LANES:]
        turned = lax.dot_general(
            had_bf, both, (((1,), (1,)), ((), ())), preferred_element_type=jnp.float32
        )
        top = jnp.max(jnp.abs(turned), axis=0, keepdims=True)
        half_core = lax.div(half, 512)
        for j in range(2):
            row = half_core * (peaks[seg].shape[0] // 2) + (2 * i + j)
            peaks[seg][pl.ds(row, 1), :] = top[:, j * LANES : (j + 1) * LANES]

    def peak_send(seg, partners_of, arrivals):
        return [
            copies.start(peaks[seg], arrivals.at[seg, slot, pl.ds(0, peaks[seg].shape[0])], here.near(*moves))
            for slot, moves in enumerate(partners_of)
        ]

    def peak_take(seg, sent, arrivals):
        for copy in sent:
            copy.wait_recv()
            copy.wait_send()
        best = peaks[seg][...]
        for slot in range(len(sent)):
            best = jnp.maximum(best, arrivals[seg, slot, pl.ds(0, peaks[seg].shape[0]), :])
        peaks[seg][...] = best

    eye = lax.broadcasted_iota(jnp.int32, (LANES, LANES), 0) == lax.broadcasted_iota(
        jnp.int32, (LANES, LANES), 1
    )
    ones = jnp.ones((3 * LANES, LANES), jnp.bfloat16)

    def spread(seg):
        top = peaks[seg][...]
        whole = jnp.floor(top * (1.0 / 256.0))
        ratio = 32.0 / jnp.maximum(top, 1.0)
        near1 = ratio.astype(jnp.bfloat16).astype(jnp.float32)
        near2 = (ratio - near1).astype(jnp.bfloat16).astype(jnp.float32)
        parts = (whole * 8.0, (top - whole * 256.0) * (1.0 / 32.0), near1, near2, (ratio - near1) - near2)
        first, size = SEGMENTS[seg]
        padded = peaks[seg].shape[0] // 2
        for half in range(2):
            for r in range(size // 32):
                row = half * padded + r
                diag = [
                    jnp.where(eye, jnp.broadcast_to(part[row : row + 1, :], (LANES, LANES)), 0.0).astype(
                        jnp.bfloat16
                    )
                    for part in parts
                ]
                at = pl.ds(half * 2048 + first * 4 + r * LANES, LANES)
                high_all[at, :] = jnp.dot(diag[0], ones[:LANES], preferred_element_type=jnp.float32)
                low_all[at, :] = jnp.dot(diag[1], ones[:LANES], preferred_element_type=jnp.float32)
                ratio_all[at, :] = jnp.dot(
                    jnp.concatenate(diag[2:], axis=1), ones, preferred_element_type=jnp.float32
                )

    def quantize(peak_row, gap_table, point_table, sibling_row=None):
        keys = [(r, m, p) for r in range(PEAK_ROWS) for m in range(16) for p in (0, 1)]
        batches = [keys[i : i + BATCH] for i in range(0, len(keys), BATCH)]
        held = {}

        def find_cells(batch):
            for r, m, p in batch:
                at = rows_of((peak_row + r) * 16 + m, 1)
                value = (coef_even, coef_odd)[p][at, :]
                place = jnp.minimum((value * ratio_all[at, :] + 32.0).astype(jnp.int32), 63)
                held[r, m, p] = (value, place, take(gap_table, place))

        def round_cells(batch):
            for r, m, p in batch:
                at = rows_of((peak_row + r) * 16 + m, 1)
                value, place, packed = held[r, m, p]
                offset = dither_v[pl.ds((peak_row + r) * 256 + (16 * m + p), UNIT, stride=2), :]
                whole = jnp.floor(packed)
                bound = whole + offset.astype(jnp.float32) * (packed - whole)
                up = (value - high_all[at, :] * bound) > low_all[at, :] * bound
                held[r, m, p] = take(point_table, jnp.where(up, place + 64, place))

        def store(batch):
            for r, m, p in batch:
                code = held.pop((r, m, p))
                if sibling_row is not None:
                    near = pl.ds((sibling_row + r) * 256 + (16 * m + p), UNIT, stride=2)
                    code = code + sibling_in[near, :]
                codes[pl.ds((peak_row + r) * 256 + (16 * m + p), UNIT, stride=2), :] = code

        for i in range(len(batches) + 2):
            if i < len(batches):
                find_cells(batches[i])
            if 0 <= i - 1 < len(batches):
                round_cells(batches[i - 1])
            if i >= 2:
                store(batches[i - 2])

    def tables():
        cell = (lane & 63) - 32
        low = jnp.full((UNIT, LANES), level_values[0], jnp.int32)
        high = jnp.full((UNIT, LANES), level_values[1], jnp.int32)
        low_point = jnp.full((UNIT, LANES), level_points[0], jnp.float32)
        high_point = jnp.full((UNIT, LANES), level_points[1], jnp.float32)
        for j in range(1, 15):
            passed = cell >= level_values[j]
            low = jnp.where(passed, level_values[j], low)
            high = jnp.where(passed, level_values[j + 1], high)
            low_point = jnp.where(passed, level_points[j], low_point)
            high_point = jnp.where(passed, level_points[j + 1], high_point)
        gap = low.astype(jnp.float32) + (high - low).astype(jnp.float32) * (1.0 / 64.0)
        return gap, jnp.where(lane < 64, low_point, high_point)

    halves = [None] * 3

    def quantize_other(seg, gap_table, point_table):
        first, size = SEGMENTS[seg]

        def body(r, carry):
            quantize((theirs + first) // 32 + r * PEAK_ROWS, gap_table, point_table)
            return carry

        lax.fori_loop(0, size // 32 // PEAK_ROWS, body, 0)
        halves[seg] = copies.start(
            codes.at[rows_of(theirs + first, size)], sibling_in.at[rows_of(first, size)], sibling
        )

    def quantize_own(seg, gap_table, point_table):
        first, size = SEGMENTS[seg]
        halves[seg].wait_recv()

        def body(r, carry):
            quantize(
                (mine + first) // 32 + r * PEAK_ROWS, gap_table, point_table, first // 32 + r * PEAK_ROWS
            )
            return carry

        lax.fori_loop(0, size // 32 // PEAK_ROWS, body, 0)

    places, _ = layout()
    ring = {}

    def land(seg, name, skip, count):
        return landing.at[rows_of(places[seg, name][0] + skip, count)]

    def cut(seg):
        first, size = SEGMENTS[seg]
        quarter = size // RING
        axis = ORDERS[seg][0]
        part = [mine + first + lax.rem(here.at[axis] + d, RING) * quarter for d in range(RING)]
        return quarter, quarter // 2, part, here.near((axis, 1)), here.near((axis, 3))

    def scatter_first(seg):
        quarter, low, part, right, left = cut(seg)
        high = quarter - low
        ring[seg] = [
            copies.start(codes.at[rows_of(part[2], low)], land(seg, "tl", 0, low), right),
            copies.start(codes.at[rows_of(part[2] + low, high)], land(seg, "th", 0, high), left),
            copies.start(codes.at[rows_of(part[1] + low, high)], land(seg, "fa", low, high), right),
            copies.start(codes.at[rows_of(part[3], low)], land(seg, "fb", 0, low), left),
        ]

    def scatter_second(seg):
        quarter, low, part, right, left = cut(seg)
        high = quarter - low
        waits = ring[seg]
        waits[0].wait_recv()
        add_into(codes, part[1], [(landing, places[seg, "tl"][0])], low)
        waits.append(copies.start(codes.at[rows_of(part[1], low)], land(seg, "fa", 0, low), right))
        waits[1].wait_recv()
        add_into(codes, part[3] + low, [(landing, places[seg, "th"][0])], high)
        waits.append(copies.start(codes.at[rows_of(part[3] + low, high)], land(seg, "fb", low, high), left))

    plane = {}

    def piece_at(seg, i, j):
        quarter, _, part, _, _ = cut(seg)
        _, first, second = ORDERS[seg]
        spot = lax.rem(here.at[first] + i, RING) * RING + lax.rem(here.at[second] + j, RING)
        return part[0] + spot * (quarter // 16)

    def plane_partner(seg, i, j):
        _, first, second = ORDERS[seg]
        return here.near((first, i), (second, j))

    def scatter_plane(seg):
        quarter, _, part, _, _ = cut(seg)
        for copy in ring[seg][2:]:
            copy.wait_recv()
        add_into(codes, part[0], [(landing, places[seg, "fa"][0]), (landing, places[seg, "fb"][0])], quarter)
        piece = quarter // 16
        plane[seg] = [
            copies.start(
                codes.at[rows_of(piece_at(seg, i, j), piece)],
                land(seg, "plane", (i * RING + j) * piece, piece),
                plane_partner(seg, i, j),
            )
            for i, j in PLANE
        ]

    def scatter_last(seg):
        piece = SEGMENTS[seg][1] // 64
        for copy in plane[seg]:
            copy.wait_recv()
        first = places[seg, "plane"][0]
        add_into(
            codes,
            piece_at(seg, 0, 0),
            [(landing, first + (i * RING + j) * piece) for i, j in PLANE],
            piece,
        )

    small_loads[0].wait()
    for step in range(6):
        rotate(step)
    pl.semaphore_wait(barrier, len(partners))
    sent_a = peak_send(0, PEAK_FIRST, first_in)
    for step in range(6, 12):
        rotate(step)
    peak_take(0, sent_a, first_in)
    sent_a = peak_send(0, PEAK_SECOND, second_in)
    sent_b = peak_send(1, PEAK_FIRST, first_in)
    for step in range(12, 16):
        rotate(step)
    sent_c = peak_send(2, PEAK_FIRST, first_in)
    for load in small_loads[1:]:
        load.wait()
    gap_table, point_table = tables()
    peak_take(1, sent_b, first_in)
    sent_b = peak_send(1, PEAK_SECOND, second_in)
    peak_take(2, sent_c, first_in)
    sent_c = peak_send(2, PEAK_SECOND, second_in)
    peak_take(0, sent_a, second_in)
    spread(0)
    quantize_other(0, gap_table, point_table)
    peak_take(1, sent_b, second_in)
    spread(1)
    quantize_other(1, gap_table, point_table)
    quantize_own(0, gap_table, point_table)
    scatter_first(0)
    peak_take(2, sent_c, second_in)
    spread(2)
    quantize_other(2, gap_table, point_table)
    quantize_own(1, gap_table, point_table)
    scatter_first(1)
    scatter_second(0)
    quantize_own(2, gap_table, point_table)
    scatter_first(2)
    scatter_second(1)
    scatter_plane(0)
    scatter_second(2)
    scatter_plane(1)
    scatter_plane(2)
    for seg in range(3):
        scatter_last(seg)

    units = [(seg, piece_at(seg, 0, 0) + i) for seg, (_, size) in enumerate(SEGMENTS) for i in range(size // 64)]
    for i, (_, unit) in enumerate(units):
        owned[pl.ds(i * UNIT, UNIT), :] = codes[rows_of(unit, 1), :]
    count = len(units) * UNIT // 2
    both = jnp.concatenate(
        [owned[pl.ds(0, count, stride=2), :], owned[pl.ds(1, count, stride=2), :]], axis=1
    )
    back = jnp.dot(both, had, precision=lax.Precision.HIGHEST, preferred_element_type=jnp.float32)
    owned[pl.ds(0, count, stride=2), :] = back[:, :LANES]
    owned[pl.ds(1, count, stride=2), :] = back[:, LANES:]
    for i, (seg, unit) in enumerate(units):
        wide = jnp.broadcast_to(words[pl.ds(lax.div(unit, 4), 1), :], (UNIT, LANES))
        word = take(wide, word_lane + 32 * lax.rem(unit, 4))
        spot = unit - (mine + SEGMENTS[seg][0])
        row = core * (peaks[seg].shape[0] // 2) + lax.div(spot, 32)
        wide = jnp.broadcast_to(peaks[seg][pl.ds(row, 1), :], (UNIT, LANES))
        factor = take(wide, 4 * lax.rem(spot, 32) + (sub >> 1)) * (1.0 / 2.0**29)
        grad = owned[pl.ds(i * UNIT, UNIT), :] * factor
        out[rows_of(unit, 1), :] = jnp.where((word << word_shift) < 0, -grad, grad)

    def send(start, size, to):
        at = rows_of(start, size)
        return copies.start(out.at[at], out.at[at], to)

    last = []
    gather = {}
    arrive = {}

    def gather_plane(seg):
        piece = SEGMENTS[seg][1] // 64
        for i, j in PLANE:
            arrive.setdefault((seg, (RING - i) % RING), []).append(
                send(piece_at(seg, 0, 0), piece, plane_partner(seg, i, j))
            )

    def group_of(seg, i):
        quarter, _, part, right, left = cut(seg)
        size = quarter // RING
        skip = lax.rem(here.at[ORDERS[seg][1]] + i, RING) * size
        return size, size // 2, [start + skip for start in part], right, left

    def gather_first(seg, i):
        for copy in arrive[seg, i]:
            copy.wait_recv()
        size, low, part, right, left = group_of(seg, i)
        high = size - low
        gather[seg, i] = [
            send(part[0], low, right),
            send(part[0] + low, high, left),
            send(part[0] + low, high, right),
            send(part[0], low, left),
        ]
        last.append(send(part[0], size, sibling))

    def gather_second(seg, i):
        size, low, part, right, left = group_of(seg, i)
        high = size - low
        waits = gather[seg, i]
        waits[0].wait_recv()
        waits.append(send(part[3], low, right))
        waits[1].wait_recv()
        waits.append(send(part[1] + low, high, left))
        waits[2].wait_recv()
        waits[3].wait_recv()
        last.append(send(part[3], size, sibling))
        last.append(send(part[1], size, sibling))

    def gather_last(seg, i):
        size, _, part, _, _ = group_of(seg, i)
        for copy in gather[seg, i][4:]:
            copy.wait_recv()
        last.append(send(part[2], size, sibling))

    for seg in range(3):
        gather_plane(seg)
    for turn in range(len(GROUPS) + 2):
        if turn < len(GROUPS):
            for seg in range(3):
                gather_first(seg, GROUPS[turn])
        if 0 <= turn - 1 < len(GROUPS):
            for seg in range(3):
                gather_second(seg, GROUPS[turn - 1])
        if turn >= 2:
            for seg in range(3):
                gather_last(seg, GROUPS[turn - 2])
    for copy in last:
        copy.wait_recv()
    for copy in copies.all[3 * 22 :]:
        copy.wait_send()


def mean_gradient(gradients, dither, sign_words, level_values, level_points):
    units = layout()[1]
    whole = pltpu.VMEM((ROWS, LANES), jnp.float32)
    half = pltpu.VMEM((HALF_ROWS, LANES), jnp.float32)
    anywhere = pl.BlockSpec(memory_space=pltpu.HBM)
    return pl.pallas_call(
        reduce_kernel,
        out_shape=jax.ShapeDtypeStruct((ROWS, LANES), jnp.float32),
        in_specs=[anywhere] * 5,
        out_specs=pl.BlockSpec(memory_space=pltpu.VMEM),
        scratch_shapes=[
            pltpu.VMEM((1, ROWS * LANES), jnp.bfloat16),
            pltpu.VMEM((ROWS, LANES), jnp.int32),
            pltpu.VMEM((ROWS // 32, LANES), jnp.int32),
            pltpu.SMEM((16,), jnp.int32),
            pltpu.SMEM((16,), jnp.float32),
            pltpu.VMEM((CHUNK, LANES), jnp.float32),
            half,
            half,
            whole,
            pltpu.VMEM((16, LANES), jnp.float32),
            pltpu.VMEM((16, LANES), jnp.float32),
            pltpu.VMEM((8, LANES), jnp.float32),
            pltpu.VMEM((3, 7, 16, LANES), jnp.float32),
            pltpu.VMEM((3, 15, 16, LANES), jnp.float32),
            half,
            half,
            half,
            half,
            pltpu.VMEM((units * UNIT, LANES), jnp.float32),
            pltpu.VMEM((64, LANES), jnp.float32),
            pltpu.SemaphoreType.DMA((COPIES,)),
            pltpu.SemaphoreType.DMA((COPIES,)),
            pltpu.SemaphoreType.DMA((ROWS // CHUNK,)),
            pltpu.SemaphoreType.DMA((4,)),
        ],
        compiler_params=pltpu.CompilerParams(
            collective_id=0, has_side_effects=True, vmem_limit_bytes=47 * 2**20
        ),
        cost_estimate=pl.CostEstimate(flops=2**31, bytes_accessed=12 * 2**20, transcendentals=0),
    )(
        gradients,
        dither.reshape(ROWS, LANES),
        sign_words.reshape(-1, LANES),
        level_values,
        level_points,
    )


def body(
    gradients, dither, sign_words, level_values, level_points, params, first_moment, second_moment
):
    mean_grad = mean_gradient(gradients, dither, sign_words, level_values, level_points).reshape(-1)
    new_first = beta_first * first_moment + (1.0 - beta_first) * mean_grad
    new_second = beta_second * second_moment + (1.0 - beta_second) * mean_grad * mean_grad
    update = new_first / bias_first / (jnp.sqrt(new_second / bias_second) + epsilon)
    new_params = params - step_rate * update
    return (new_params, new_first, new_second, update)


def solution(mesh):
    placed = (P(("dp", "outer"), None), P(("dp", "outer"), None), P(), P(), P(), P(), P(), P())
    return jax.shard_map(
        body, mesh=mesh, in_specs=placed, out_specs=(P(), P(), P(), P()), check_vma=False
    )
```

```python
import jax
import jax.numpy as jnp
from jax import lax
from jax.experimental import pallas as pl
from jax.experimental.pallas import tpu as pltpu
from jax.sharding import PartitionSpec as P

MESH = pl.DeviceIdType.MESH
LANES = 128
UNIT = 8
ROWS = 8192
HALF_ROWS = ROWS // 2
CHUNK = 512
RING = 4
SEGMENTS = ((0, 192), (192, 192), (384, 128))
ORDERS = (("x", "y", "z"), ("y", "z", "x"), ("z", "x", "y"))
GROUPS = (0, 1, 3, 2)
PLANE = tuple((i, j) for i in (2, 1, 3, 0) for j in (2, 1, 3, 0) if i + j)
BATCH = 16
STEP_ROWS = (3, 3, 2)

beta_first = 0.9
beta_second = 0.95
bias_first = 1.0 - 0.9**50
bias_second = 1.0 - 0.95**50
epsilon = 1e-08
step_rate = 0.01


def rows_of(start, count):
    return pl.ds(pl.multiple_of(start * UNIT, UNIT), count * UNIT)


def take(table, idx):
    return jnp.take_along_axis(table, idx, axis=1, mode="promise_in_bounds")


def hadamard_128(length):
    common = lax.broadcasted_iota(jnp.int32, (length, length), 0) & lax.broadcasted_iota(
        jnp.int32, (length, length), 1
    )
    for shift in (4, 2, 1):
        common = common ^ (common >> shift)
    return jnp.where((common & 1) == 1, -128.0, 128.0).astype(jnp.float32)


class Place:
    def __init__(self):
        dp, outer = lax.axis_index("dp"), lax.axis_index("outer")
        self.at = {
            "y": lax.div(dp, 8),
            "x": lax.rem(lax.div(dp, 4), 2) * 2 + lax.div(outer, 2),
            "z": lax.rem(dp, 4),
            "core": lax.rem(outer, 2),
        }

    def near(self, *moves):
        at = dict(self.at)
        for axis, delta in moves:
            at[axis] = lax.rem(at[axis] + delta, 2 if axis == "core" else RING)
        dp = at["y"] * 8 + lax.div(at["x"], 2) * 4 + at["z"]
        return {"dp": dp, "outer": lax.rem(at["x"], 2) * 2 + at["core"]}


class Copies:
    def __init__(self, send, recv):
        self.send, self.recv, self.all = send, recv, []

    def start(self, src, dst, to):
        copy = pltpu.make_async_remote_copy(
            src_ref=src,
            dst_ref=dst,
            send_sem=self.send.at[len(self.all)],
            recv_sem=self.recv.at[len(self.all)],
            device_id=to,
            device_id_type=MESH,
        )
        self.all.append(copy)
        copy.start()
        return copy


PEAK_ROUNDS = (
    tuple((("x", i), ("core", j)) for i in (2, 1, 3, 0) for j in (1, 0) if i + j),
    tuple((("y", i),) for i in (2, 1, 3)),
    tuple((("z", i),) for i in (2, 1, 3)),
)
PEAK_FIRST_SLOT = (0, 7, 10)
PEAK_COPIES = 13
COPIES = 3 * (PEAK_COPIES + 1 + 6 + 15 + 15 + 4 * 10)


def layout():
    places, used = {}, 0
    for seg, (_, size) in enumerate(SEGMENTS):
        quarter = size // RING
        low = quarter // 2
        for name, count in (
            ("tl", low),
            ("th", quarter - low),
            ("fa", quarter),
            ("fb", quarter),
            ("plane", quarter),
        ):
            places[seg, name] = (used, count)
            used += count
    return places, used


def add_into(dst, start, sources, count):
    step = 8 if count % 8 == 0 and count > 12 else count

    def body(i, carry):
        here = rows_of(start + i * step, step)
        value = dst[here, :]
        for ref, first in sources:
            value = value + ref[rows_of(first + i * step, step), :]
        dst[here, :] = value
        return carry

    if step == count:
        body(0, 0)
    else:
        lax.fori_loop(0, count // step, body, 0)


def reduce_kernel(
    grad_hbm, dither_hbm, words_hbm, values_hbm, points_hbm, out,
    grad_v, dither_v, words, level_values, level_points, signed, coef_even, coef_odd, codes,
    peak_a, peak_b, peak_c, peak_in, high_all, low_all, ratio_all,
    sibling_in, landing, owned, send_sems, recv_sems, grad_sems, load_sems,
):
    here = Place()
    core = here.at["core"]
    copies = Copies(send_sems, recv_sems)
    peaks = (peak_a, peak_b, peak_c)
    sibling = here.near(("core", 1))
    mine, theirs = core * 512, (1 - core) * 512

    barrier = pltpu.get_barrier_semaphore()
    partners = [here.near(*moves) for moves in PEAK_ROUNDS[0] + PEAK_ROUNDS[1] + PEAK_ROUNDS[2]]
    for partner in partners:
        pl.semaphore_signal(barrier, inc=1, device_id=partner, device_id_type=MESH)

    small_loads = [
        pltpu.make_async_copy(src, dst, load_sems.at[i])
        for i, (src, dst) in enumerate(
            ((words_hbm, words), (values_hbm, level_values), (points_hbm, level_points), (dither_hbm, dither_v))
        )
    ]
    span = CHUNK * LANES
    small_loads[0].start()
    steps = []
    for seg, (first, size) in enumerate(SEGMENTS):
        for half in (theirs, mine):
            steps += [(seg, half, (half + first) // 64 + i, i) for i in range(size // 64)]
    loads = []
    for i, (_, _, chunk, _) in enumerate(steps):
        at = pl.ds(pl.multiple_of(chunk * span, span), span)
        loads.append(pltpu.make_async_copy(grad_hbm.at[:, at], grad_v.at[:, at], grad_sems.at[i]))
        loads[-1].start()
    for load in small_loads[1:3]:
        load.start()

    lane = lax.broadcasted_iota(jnp.int32, (UNIT, LANES), 1)
    sub = lax.broadcasted_iota(jnp.int32, (UNIT, LANES), 0)
    word_lane = sub * 4 + (lane >> 5)
    word_shift = 31 - (lane & 31)
    had = hadamard_128(2 * LANES)
    had_bf = had.astype(jnp.bfloat16)
    for ref in peaks:
        ref[...] = jnp.zeros_like(ref)

    def sign_chunk(chunk, slot):
        for r in range(CHUNK // 32):
            word_row = chunk * (CHUNK // 32) + r
            wide = jnp.broadcast_to(words[pl.ds(word_row, 1), :], (UNIT, LANES))
            for k in range(4):
                word = take(wide, word_lane + 32 * k)
                first = pl.multiple_of(word_row * 4096 + k * 1024, 1024)
                grad = grad_v[:, pl.ds(first, 1024)].astype(jnp.float32).reshape(UNIT, LANES)
                signed[slot, rows_of(r * 4 + k, 1), :] = jnp.where((word << word_shift) < 0, -grad, grad)

    def rotate_chunk(seg, half_core, i, chunk, slot):
        even = signed[slot, pl.ds(0, CHUNK // 2, stride=2), :]
        odd = signed[slot, pl.ds(1, CHUNK // 2, stride=2), :]
        both = jnp.concatenate([even, odd], axis=1).astype(jnp.bfloat16)
        coeffs = jnp.dot(both, had_bf, preferred_element_type=jnp.float32)
        at = rows_of(chunk * 32, 32)
        coef_even[at, :] = coeffs[:, :LANES]
        coef_odd[at, :] = coeffs[:, LANES:]
        turned = lax.dot_general(
            had_bf, both, (((1,), (1,)), ((), ())), preferred_element_type=jnp.float32
        )
        top = jnp.max(jnp.abs(turned), axis=0, keepdims=True)
        for j in range(2):
            row = half_core * (peaks[seg].shape[0] // 2) + (2 * i + j)
            peaks[seg][pl.ds(row, 1), :] = top[:, j * LANES : (j + 1) * LANES]

    def rotate(seg):
        first, size = SEGMENTS[seg]
        count = size // 64
        for (step_seg, *_), load in zip(steps, loads, strict=True):
            if step_seg == seg:
                load.wait()

        def body(h, carry):
            half_core = (1 - core) + h * (2 * core - 1)
            start = half_core * 8 + first // 64
            for i in range(count + 1):
                if i < count:
                    sign_chunk(start + i, i % 2)
                if i >= 1:
                    rotate_chunk(seg, half_core, i - 1, start + i - 1, (i - 1) % 2)
            return carry

        lax.fori_loop(0, 2, body, 0)

    sent_peaks = {}

    def peak_send(seg, turn):
        size = peaks[seg].shape[0]
        sent_peaks[seg, turn] = [
            copies.start(
                peaks[seg],
                peak_in.at[seg, PEAK_FIRST_SLOT[turn] + slot, pl.ds(0, size)],
                here.near(*moves),
            )
            for slot, moves in enumerate(PEAK_ROUNDS[turn])
        ]

    def peak_take(seg, turn):
        for copy in sent_peaks[seg, turn]:
            copy.wait_recv()
            copy.wait_send()
        best = peaks[seg][...]
        for slot in range(len(PEAK_ROUNDS[turn])):
            arrived = peak_in[seg, PEAK_FIRST_SLOT[turn] + slot, pl.ds(0, peaks[seg].shape[0]), :]
            best = jnp.maximum(best, arrived)
        peaks[seg][...] = best

    eye = lax.broadcasted_iota(jnp.int32, (LANES, LANES), 0) == lax.broadcasted_iota(
        jnp.int32, (LANES, LANES), 1
    )
    ones = jnp.ones((3 * LANES, LANES), jnp.bfloat16)

    def spread(seg):
        top = peaks[seg][...]
        whole = jnp.floor(top * (1.0 / 256.0))
        ratio = 32.0 / jnp.maximum(top, 1.0)
        near1 = ratio.astype(jnp.bfloat16).astype(jnp.float32)
        near2 = (ratio - near1).astype(jnp.bfloat16).astype(jnp.float32)
        parts = (whole * 8.0, (top - whole * 256.0) * (1.0 / 32.0), near1, near2, (ratio - near1) - near2)
        first, size = SEGMENTS[seg]
        padded = peaks[seg].shape[0] // 2
        for half in range(2):
            for r in range(size // 32):
                row = half * padded + r
                diag = [
                    jnp.where(eye, jnp.broadcast_to(part[row : row + 1, :], (LANES, LANES)), 0.0).astype(
                        jnp.bfloat16
                    )
                    for part in parts
                ]
                at = pl.ds(half * 2048 + first * 4 + r * LANES, LANES)
                high_all[at, :] = jnp.dot(diag[0], ones[:LANES], preferred_element_type=jnp.float32)
                low_all[at, :] = jnp.dot(diag[1], ones[:LANES], preferred_element_type=jnp.float32)
                ratio_all[at, :] = jnp.dot(
                    jnp.concatenate(diag[2:], axis=1), ones, preferred_element_type=jnp.float32
                )

    def quantize(count, peak_row, gap_table, point_table, sibling_row=None):
        keys = [(r, m, p) for r in range(count) for m in range(16) for p in (0, 1)]
        batches = [keys[i : i + BATCH] for i in range(0, len(keys), BATCH)]
        held = {}

        def find_cells(batch):
            for r, m, p in batch:
                at = rows_of((peak_row + r) * 16 + m, 1)
                value = (coef_even, coef_odd)[p][at, :]
                place = jnp.minimum((value * ratio_all[at, :] + 32.0).astype(jnp.int32), 63)
                held[r, m, p] = (value, place, take(gap_table, place))

        def round_cells(batch):
            for r, m, p in batch:
                at = rows_of((peak_row + r) * 16 + m, 1)
                value, place, packed = held[r, m, p]
                offset = dither_v[pl.ds((peak_row + r) * 256 + (16 * m + p), UNIT, stride=2), :]
                whole = jnp.floor(packed)
                bound = whole + offset.astype(jnp.float32) * (packed - whole)
                up = (value - high_all[at, :] * bound) > low_all[at, :] * bound
                held[r, m, p] = take(point_table, jnp.where(up, place + 64, place))

        def store(batch):
            for r, m, p in batch:
                code = held.pop((r, m, p))
                if sibling_row is not None:
                    near = pl.ds((sibling_row + r) * 256 + (16 * m + p), UNIT, stride=2)
                    code = code + sibling_in[near, :]
                codes[pl.ds((peak_row + r) * 256 + (16 * m + p), UNIT, stride=2), :] = code

        for i in range(len(batches) + 2):
            if i < len(batches):
                find_cells(batches[i])
            if 0 <= i - 1 < len(batches):
                round_cells(batches[i - 1])
            if i >= 2:
                store(batches[i - 2])

    def tables():
        cell = (lane & 63) - 32
        low = jnp.full((UNIT, LANES), level_values[0], jnp.int32)
        high = jnp.full((UNIT, LANES), level_values[1], jnp.int32)
        low_point = jnp.full((UNIT, LANES), level_points[0], jnp.float32)
        high_point = jnp.full((UNIT, LANES), level_points[1], jnp.float32)
        for j in range(1, 15):
            passed = cell >= level_values[j]
            low = jnp.where(passed, level_values[j], low)
            high = jnp.where(passed, level_values[j + 1], high)
            low_point = jnp.where(passed, level_points[j], low_point)
            high_point = jnp.where(passed, level_points[j + 1], high_point)
        gap = low.astype(jnp.float32) + (high - low).astype(jnp.float32) * (1.0 / 64.0)
        return gap, jnp.where(lane < 64, low_point, high_point)

    halves = [None] * 3

    def quantize_other(seg, gap_table, point_table):
        first, size = SEGMENTS[seg]
        step = STEP_ROWS[seg]

        def body(r, carry):
            quantize(step, (theirs + first) // 32 + r * step, gap_table, point_table)
            return carry

        lax.fori_loop(0, size // 32 // step, body, 0)
        halves[seg] = copies.start(
            codes.at[rows_of(theirs + first, size)], sibling_in.at[rows_of(first, size)], sibling
        )

    def quantize_own(seg, gap_table, point_table):
        first, size = SEGMENTS[seg]
        step = STEP_ROWS[seg]
        halves[seg].wait_recv()

        def body(r, carry):
            quantize(step, (mine + first) // 32 + r * step, gap_table, point_table, first // 32 + r * step)
            return carry

        lax.fori_loop(0, size // 32 // step, body, 0)

    places, _ = layout()
    ring = {}

    def land(seg, name, skip, count):
        return landing.at[rows_of(places[seg, name][0] + skip, count)]

    def cut(seg):
        first, size = SEGMENTS[seg]
        quarter = size // RING
        axis = ORDERS[seg][0]
        part = [mine + first + lax.rem(here.at[axis] + d, RING) * quarter for d in range(RING)]
        return quarter, quarter // 2, part, here.near((axis, 1)), here.near((axis, 3))

    def scatter_first(seg):
        quarter, low, part, right, left = cut(seg)
        high = quarter - low
        ring[seg] = [
            copies.start(codes.at[rows_of(part[2], low)], land(seg, "tl", 0, low), right),
            copies.start(codes.at[rows_of(part[2] + low, high)], land(seg, "th", 0, high), left),
            copies.start(codes.at[rows_of(part[1] + low, high)], land(seg, "fa", low, high), right),
            copies.start(codes.at[rows_of(part[3], low)], land(seg, "fb", 0, low), left),
        ]

    def scatter_second(seg):
        quarter, low, part, right, left = cut(seg)
        high = quarter - low
        waits = ring[seg]
        waits[0].wait_recv()
        add_into(codes, part[1], [(landing, places[seg, "tl"][0])], low)
        waits.append(copies.start(codes.at[rows_of(part[1], low)], land(seg, "fa", 0, low), right))
        waits[1].wait_recv()
        add_into(codes, part[3] + low, [(landing, places[seg, "th"][0])], high)
        waits.append(copies.start(codes.at[rows_of(part[3] + low, high)], land(seg, "fb", low, high), left))

    plane = {}

    def piece_at(seg, i, j):
        quarter, _, part, _, _ = cut(seg)
        _, first, second = ORDERS[seg]
        spot = lax.rem(here.at[first] + i, RING) * RING + lax.rem(here.at[second] + j, RING)
        return part[0] + spot * (quarter // 16)

    def plane_partner(seg, i, j):
        _, first, second = ORDERS[seg]
        return here.near((first, i), (second, j))

    def scatter_plane(seg):
        quarter, _, part, _, _ = cut(seg)
        for copy in ring[seg][2:]:
            copy.wait_recv()
        add_into(codes, part[0], [(landing, places[seg, "fa"][0]), (landing, places[seg, "fb"][0])], quarter)
        piece = quarter // 16
        plane[seg] = [
            copies.start(
                codes.at[rows_of(piece_at(seg, i, j), piece)],
                land(seg, "plane", (i * RING + j) * piece, piece),
                plane_partner(seg, i, j),
            )
            for i, j in PLANE
        ]

    def scatter_last(seg):
        piece = SEGMENTS[seg][1] // 64
        for copy in plane[seg]:
            copy.wait_recv()
        first = places[seg, "plane"][0]
        add_into(
            codes,
            piece_at(seg, 0, 0),
            [(landing, first + (i * RING + j) * piece) for i, j in PLANE],
            piece,
        )

    small_loads[0].wait()
    rotate(0)
    pl.semaphore_wait(barrier, len(partners))
    peak_send(0, 0)
    small_loads[3].start()
    rotate(1)
    peak_send(1, 0)
    rotate(2)
    peak_send(2, 0)
    for load in small_loads[1:]:
        load.wait()
    gap_table, point_table = tables()
    for turn in (0, 1):
        for seg in range(3):
            peak_take(seg, turn)
            peak_send(seg, turn + 1)
    peak_take(0, 2)
    spread(0)
    quantize_other(0, gap_table, point_table)
    peak_take(1, 2)
    spread(1)
    peak_take(2, 2)
    spread(2)
    quantize_own(0, gap_table, point_table)
    scatter_first(0)
    quantize_other(1, gap_table, point_table)
    quantize_other(2, gap_table, point_table)
    quantize_own(1, gap_table, point_table)
    scatter_first(1)
    scatter_second(0)
    quantize_own(2, gap_table, point_table)
    scatter_first(2)
    scatter_second(1)
    scatter_plane(0)
    scatter_second(2)
    scatter_plane(1)
    scatter_plane(2)
    for seg in range(3):
        scatter_last(seg)

    units = [(seg, piece_at(seg, 0, 0) + i) for seg, (_, size) in enumerate(SEGMENTS) for i in range(size // 64)]
    for i, (_, unit) in enumerate(units):
        owned[pl.ds(i * UNIT, UNIT), :] = codes[rows_of(unit, 1), :]
    count = len(units) * UNIT // 2
    both = jnp.concatenate(
        [owned[pl.ds(0, count, stride=2), :], owned[pl.ds(1, count, stride=2), :]], axis=1
    )
    back = jnp.dot(both, had, precision=lax.Precision.HIGHEST, preferred_element_type=jnp.float32)
    owned[pl.ds(0, count, stride=2), :] = back[:, :LANES]
    owned[pl.ds(1, count, stride=2), :] = back[:, LANES:]
    for i, (seg, unit) in enumerate(units):
        wide = jnp.broadcast_to(words[pl.ds(lax.div(unit, 4), 1), :], (UNIT, LANES))
        word = take(wide, word_lane + 32 * lax.rem(unit, 4))
        spot = unit - (mine + SEGMENTS[seg][0])
        row = core * (peaks[seg].shape[0] // 2) + lax.div(spot, 32)
        wide = jnp.broadcast_to(peaks[seg][pl.ds(row, 1), :], (UNIT, LANES))
        factor = take(wide, 4 * lax.rem(spot, 32) + (sub >> 1)) * (1.0 / 2.0**29)
        grad = owned[pl.ds(i * UNIT, UNIT), :] * factor
        out[rows_of(unit, 1), :] = jnp.where((word << word_shift) < 0, -grad, grad)

    def send(start, size, to):
        at = rows_of(start, size)
        return copies.start(out.at[at], out.at[at], to)

    last = []
    gather = {}
    arrive = {}

    def gather_plane(seg, i):
        piece = SEGMENTS[seg][1] // 64
        for j in (2, 1, 3, 0):
            if i + j:
                arrive.setdefault((seg, (RING - i) % RING), []).append(
                    send(piece_at(seg, 0, 0), piece, plane_partner(seg, i, j))
                )

    def group_of(seg, i):
        quarter, _, part, right, left = cut(seg)
        size = quarter // RING
        skip = lax.rem(here.at[ORDERS[seg][1]] + i, RING) * size
        return size, size // 2, [start + skip for start in part], right, left

    def gather_first(seg, i):
        for copy in arrive[seg, i]:
            copy.wait_recv()
        size, low, part, right, left = group_of(seg, i)
        high = size - low
        gather[seg, i] = [
            send(part[0], low, right),
            send(part[0] + low, high, left),
            send(part[0] + low, high, right),
            send(part[0], low, left),
        ]
        last.append(send(part[0], size, sibling))

    def gather_second(seg, i):
        size, low, part, right, left = group_of(seg, i)
        high = size - low
        waits = gather[seg, i]
        waits[0].wait_recv()
        waits.append(send(part[3], low, right))
        waits[1].wait_recv()
        waits.append(send(part[1] + low, high, left))
        waits[2].wait_recv()
        waits[3].wait_recv()
        last.append(send(part[3], size, sibling))
        last.append(send(part[1], size, sibling))

    def gather_last(seg, i):
        size, _, part, _, _ = group_of(seg, i)
        for copy in gather[seg, i][4:]:
            copy.wait_recv()
        last.append(send(part[2], size, sibling))

    for i in GROUPS:
        for seg in range(3):
            gather_plane(seg, i)
    for turn in range(len(GROUPS) + 2):
        if turn < len(GROUPS):
            for seg in range(3):
                gather_first(seg, GROUPS[turn])
        if 0 <= turn - 1 < len(GROUPS):
            for seg in range(3):
                gather_second(seg, GROUPS[turn - 1])
        if turn >= 2:
            for seg in range(3):
                gather_last(seg, GROUPS[turn - 2])
    for copy in last:
        copy.wait_recv()
    for copy in copies.all[3 * PEAK_COPIES :]:
        copy.wait_send()


def mean_gradient(gradients, dither, sign_words, level_values, level_points):
    units = layout()[1]
    whole = pltpu.VMEM((ROWS, LANES), jnp.float32)
    half = pltpu.VMEM((HALF_ROWS, LANES), jnp.float32)
    anywhere = pl.BlockSpec(memory_space=pltpu.HBM)
    return pl.pallas_call(
        reduce_kernel,
        out_shape=jax.ShapeDtypeStruct((ROWS, LANES), jnp.float32),
        in_specs=[anywhere] * 5,
        out_specs=pl.BlockSpec(memory_space=pltpu.VMEM),
        scratch_shapes=[
            pltpu.VMEM((1, ROWS * LANES), jnp.bfloat16),
            pltpu.VMEM((ROWS, LANES), jnp.int32),
            pltpu.VMEM((ROWS // 32, LANES), jnp.int32),
            pltpu.SMEM((16,), jnp.int32),
            pltpu.SMEM((16,), jnp.float32),
            pltpu.VMEM((2, CHUNK, LANES), jnp.float32),
            half,
            half,
            whole,
            pltpu.VMEM((16, LANES), jnp.float32),
            pltpu.VMEM((16, LANES), jnp.float32),
            pltpu.VMEM((8, LANES), jnp.float32),
            pltpu.VMEM((3, PEAK_COPIES, 16, LANES), jnp.float32),
            half,
            half,
            half,
            half,
            pltpu.VMEM((units * UNIT, LANES), jnp.float32),
            pltpu.VMEM((64, LANES), jnp.float32),
            pltpu.SemaphoreType.DMA((COPIES,)),
            pltpu.SemaphoreType.DMA((COPIES,)),
            pltpu.SemaphoreType.DMA((ROWS // CHUNK,)),
            pltpu.SemaphoreType.DMA((4,)),
        ],
        compiler_params=pltpu.CompilerParams(
            collective_id=0, has_side_effects=True, vmem_limit_bytes=47 * 2**20
        ),
        cost_estimate=pl.CostEstimate(flops=2**31, bytes_accessed=12 * 2**20, transcendentals=0),
    )(
        gradients,
        dither.reshape(ROWS, LANES),
        sign_words.reshape(-1, LANES),
        level_values,
        level_points,
    )


def body(
    gradients, dither, sign_words, level_values, level_points, params, first_moment, second_moment
):
    mean_grad = mean_gradient(gradients, dither, sign_words, level_values, level_points).reshape(-1)
    new_first = beta_first * first_moment + (1.0 - beta_first) * mean_grad
    new_second = beta_second * second_moment + (1.0 - beta_second) * mean_grad * mean_grad
    update = new_first * (1.0 / bias_first) / (jnp.sqrt(new_second * (1.0 / bias_second)) + epsilon)
    new_params = params - step_rate * update
    return (new_params, new_first, new_second, update)


def solution(mesh):
    placed = (P(("dp", "outer"), None), P(("dp", "outer"), None), P(), P(), P(), P(), P(), P())
    return jax.shard_map(
        body, mesh=mesh, in_specs=placed, out_specs=(P(), P(), P(), P()), check_vma=False
    )
```

```python
import jax
import jax.numpy as jnp
from jax import lax
from jax.experimental import pallas as pl
from jax.experimental.pallas import tpu as pltpu
from jax.sharding import PartitionSpec as P

MESH = pl.DeviceIdType.MESH
LANES = 128
UNIT = 8
ROWS = 8192
CHUNK = 512
RING = 4
PARTS = 8
ORDERS = (("x", "y", "z"), ("y", "z", "x"), ("z", "x", "y"))
MEMBERS = ((0, 3), (3, 3), (6, 2))
WAVES = ((0, 3, 6), (1, 4, 7), (2, 5))
QUARTER = 16
GROUPS = (0, 1, 3, 2)
PLANE = tuple((i, j) for i in (2, 1, 3, 0) for j in (2, 1, 3, 0) if i + j)
BATCH = 16

beta_first = 0.9
beta_second = 0.95
bias_first = 1.0 - 0.9**50
bias_second = 1.0 - 0.95**50
epsilon = 1e-08
step_rate = 0.01


def rows_of(start, count):
    return pl.ds(pl.multiple_of(start * UNIT, UNIT), count * UNIT)


def take(table, idx):
    return jnp.take_along_axis(table, idx, axis=1, mode="promise_in_bounds")


def hadamard_128(length):
    common = lax.broadcasted_iota(jnp.int32, (length, length), 0) & lax.broadcasted_iota(
        jnp.int32, (length, length), 1
    )
    for shift in (4, 2, 1):
        common = common ^ (common >> shift)
    return jnp.where((common & 1) == 1, -128.0, 128.0).astype(jnp.float32)


class Place:
    def __init__(self):
        dp, outer = lax.axis_index("dp"), lax.axis_index("outer")
        self.at = {
            "y": lax.div(dp, 8),
            "x": lax.rem(lax.div(dp, 4), 2) * 2 + lax.div(outer, 2),
            "z": lax.rem(dp, 4),
            "core": lax.rem(outer, 2),
        }

    def near(self, *moves):
        at = dict(self.at)
        for axis, delta in moves:
            at[axis] = lax.rem(at[axis] + delta, 2 if axis == "core" else RING)
        dp = at["y"] * 8 + lax.div(at["x"], 2) * 4 + at["z"]
        return {"dp": dp, "outer": lax.rem(at["x"], 2) * 2 + at["core"]}


class Copies:
    def __init__(self, send, recv):
        self.send, self.recv, self.used, self.late = send, recv, 0, []

    def start(self, src, dst, to, late=True):
        copy = pltpu.make_async_remote_copy(
            src_ref=src,
            dst_ref=dst,
            send_sem=self.send.at[self.used],
            recv_sem=self.recv.at[self.used],
            device_id=to,
            device_id_type=MESH,
        )
        self.used += 1
        if late:
            self.late.append(copy)
        copy.start()
        return copy


PEAK_ROUNDS = (
    tuple((("x", i), ("core", j)) for i in (2, 1, 3, 0) for j in (1, 0) if i + j),
    tuple((("y", i),) for i in (2, 1, 3)),
    tuple((("z", i),) for i in (2, 1, 3)),
)
PEAK_FIRST_SLOT = (0, 7, 10)
PEAK_COPIES = 13
COPIES = 3 * PEAK_COPIES + 1 + PARTS * (2 + 6 + 15) + 3 * (15 + 4 * 10)


LANDING = {"tl": 0, "th": 8, "fa": 16, "fb": 32, "plane": 48}
LANDING_UNITS = 64


def add_into(dst, part, start, landing, firsts, count):
    here = rows_of(start, count)
    value = dst[part, here, :]
    for first in firsts:
        value = value + landing[part, rows_of(first, count), :]
    dst[part, here, :] = value


def reduce_kernel(
    grad_hbm, dither_hbm, words_hbm, values_hbm, points_hbm, out,
    grad_v, dither_v, words, level_values, level_points, signed, coef_even, coef_odd, codes,
    peak_a, peak_b, peak_c, peak_in, high_all, low_all, ratio_all,
    near_even, near_odd, near_dither, landing, owned, send_sems, recv_sems, grad_sems, load_sems,
):
    here = Place()
    core = here.at["core"]
    copies = Copies(send_sems, recv_sems)
    peaks = (peak_a, peak_b, peak_c)
    sibling = here.near(("core", 1))
    mine, theirs = core * PARTS, (1 - core) * PARTS

    barrier = pltpu.get_barrier_semaphore()
    partners = [here.near(*moves) for moves in PEAK_ROUNDS[0] + PEAK_ROUNDS[1] + PEAK_ROUNDS[2]]
    for partner in partners:
        pl.semaphore_signal(barrier, inc=1, device_id=partner, device_id_type=MESH)

    small_loads = [
        pltpu.make_async_copy(src, dst, load_sems.at[i])
        for i, (src, dst) in enumerate(
            (
                (words_hbm, words),
                (values_hbm, level_values),
                (points_hbm, level_points),
                (dither_hbm.at[pl.ds(mine, PARTS)], dither_v),
            )
        )
    ]
    small_loads[0].start()
    span = CHUNK * LANES
    loads = [[] for _ in WAVES]
    for wave, parts in enumerate(WAVES):
        for i, part in enumerate(parts):
            for j, half in enumerate((theirs, mine)):
                at = pl.ds(pl.multiple_of((half + part) * span, span), span)
                loads[wave].append(
                    pltpu.make_async_copy(grad_hbm.at[:, at], grad_v.at[:, at], grad_sems.at[part * 2 + j])
                )
                loads[wave][-1].start()
    for load in small_loads[1:3]:
        load.start()

    lane = lax.broadcasted_iota(jnp.int32, (UNIT, LANES), 1)
    sub = lax.broadcasted_iota(jnp.int32, (UNIT, LANES), 0)
    word_lane = sub * 4 + (lane >> 5)
    word_shift = 31 - (lane & 31)
    had = hadamard_128(2 * LANES)
    had_bf = had.astype(jnp.bfloat16)
    for ref in peaks:
        ref[...] = jnp.zeros_like(ref)

    def sign_chunk(chunk, slot):
        for r in range(CHUNK // 32):
            word_row = chunk * (CHUNK // 32) + r
            wide = jnp.broadcast_to(words[pl.ds(word_row, 1), :], (UNIT, LANES))
            for k in range(4):
                word = take(wide, word_lane + 32 * k)
                first = pl.multiple_of(word_row * 4096 + k * 1024, 1024)
                grad = grad_v[:, pl.ds(first, 1024)].astype(jnp.float32).reshape(UNIT, LANES)
                signed[slot, rows_of(r * 4 + k, 1), :] = jnp.where((word << word_shift) < 0, -grad, grad)

    def rotate_chunk(wave, half_core, i, chunk, slot):
        even = signed[slot, pl.ds(0, CHUNK // 2, stride=2), :]
        odd = signed[slot, pl.ds(1, CHUNK // 2, stride=2), :]
        both = jnp.concatenate([even, odd], axis=1).astype(jnp.bfloat16)
        coeffs = jnp.dot(both, had_bf, preferred_element_type=jnp.float32)
        coef_even[chunk] = coeffs[:, :LANES]
        coef_odd[chunk] = coeffs[:, LANES:]
        turned = lax.dot_general(
            had_bf, both, (((1,), (1,)), ((), ())), preferred_element_type=jnp.float32
        )
        top = jnp.max(jnp.abs(turned), axis=0, keepdims=True)
        for j in range(2):
            peaks[wave][pl.ds(half_core * 8 + (2 * i + j), 1), :] = top[:, j * LANES : (j + 1) * LANES]

    def rotate(wave):
        for load in loads[wave]:
            load.wait()
        parts = WAVES[wave]

        def body(h, carry):
            half_core = (1 - core) + h * (2 * core - 1)
            for i in range(len(parts) + 1):
                if i < len(parts):
                    sign_chunk(half_core * PARTS + parts[i], i % 2)
                if i >= 1:
                    rotate_chunk(wave, half_core, i - 1, half_core * PARTS + parts[i - 1], (i - 1) % 2)
            return carry

        lax.fori_loop(0, 2, body, 0)

    near_copies = {}

    def share(wave):
        near_copies[wave] = []
        for part in WAVES[wave]:
            for src, dst in ((coef_even, near_even), (coef_odd, near_odd)):
                near_copies[wave].append(copies.start(src.at[theirs + part], dst.at[part], sibling))

    sent_peaks = {}

    def peak_send(wave, turn):
        sent_peaks[wave, turn] = [
            copies.start(
                peaks[wave], peak_in.at[wave, PEAK_FIRST_SLOT[turn] + slot], here.near(*moves), late=False
            )
            for slot, moves in enumerate(PEAK_ROUNDS[turn])
        ]

    def peak_take(wave, turn):
        for copy in sent_peaks[wave, turn]:
            copy.wait_recv()
            copy.wait_send()
        best = peaks[wave][...]
        for slot in range(len(PEAK_ROUNDS[turn])):
            best = jnp.maximum(best, peak_in[wave, PEAK_FIRST_SLOT[turn] + slot])
        peaks[wave][...] = best

    eye = lax.broadcasted_iota(jnp.int32, (LANES, LANES), 0) == lax.broadcasted_iota(
        jnp.int32, (LANES, LANES), 1
    )
    ones = jnp.ones((3 * LANES, LANES), jnp.bfloat16)

    def spread(wave):
        top = peaks[wave][rows_of(core, 1), :]
        whole = jnp.floor(top * (1.0 / 256.0))
        ratio = 32.0 / jnp.maximum(top, 1.0)
        near1 = ratio.astype(jnp.bfloat16).astype(jnp.float32)
        near2 = (ratio - near1).astype(jnp.bfloat16).astype(jnp.float32)
        pieces = (whole * 8.0, (top - whole * 256.0) * (1.0 / 32.0), near1, near2, (ratio - near1) - near2)
        for i, part in enumerate(WAVES[wave]):
            for j in range(2):
                row = 2 * i + j
                diag = [
                    jnp.where(eye, jnp.broadcast_to(piece[row : row + 1, :], (LANES, LANES)), 0.0).astype(
                        jnp.bfloat16
                    )
                    for piece in pieces
                ]
                at = pl.ds(j * LANES, LANES)
                high_all[part, at, :] = jnp.dot(diag[0], ones[:LANES], preferred_element_type=jnp.float32)
                low_all[part, at, :] = jnp.dot(diag[1], ones[:LANES], preferred_element_type=jnp.float32)
                ratio_all[part, at, :] = jnp.dot(
                    jnp.concatenate(diag[2:], axis=1), ones, preferred_element_type=jnp.float32
                )

    def tables():
        cell = (lane & 63) - 32
        low = jnp.full((UNIT, LANES), level_values[0], jnp.int32)
        high = jnp.full((UNIT, LANES), level_values[1], jnp.int32)
        low_point = jnp.full((UNIT, LANES), level_points[0], jnp.float32)
        high_point = jnp.full((UNIT, LANES), level_points[1], jnp.float32)
        for j in range(1, 15):
            passed = cell >= level_values[j]
            low = jnp.where(passed, level_values[j], low)
            high = jnp.where(passed, level_values[j + 1], high)
            low_point = jnp.where(passed, level_points[j], low_point)
            high_point = jnp.where(passed, level_points[j + 1], high_point)
        gap = low.astype(jnp.float32) + (high - low).astype(jnp.float32) * (1.0 / 64.0)
        return gap, jnp.where(lane < 64, low_point, high_point)

    def quantize_chunk(part, gap_table, point_table):
        keys = [(m, p, own) for m in range(CHUNK // 16) for p in (0, 1) for own in (True, False)]
        batches = [keys[i : i + BATCH] for i in range(0, len(keys), BATCH)]
        held = {}

        def find_cells(batch):
            for m, p, own in batch:
                at = rows_of(m, 1)
                if own:
                    value = (coef_even, coef_odd)[p][mine + part, at, :]
                else:
                    value = (near_even, near_odd)[p][part, at, :]
                place = jnp.minimum((value * ratio_all[part, at, :] + 32.0).astype(jnp.int32), 63)
                held[m, p, own] = (value, place, take(gap_table, place))

        def round_cells(batch):
            for m, p, own in batch:
                at = rows_of(m, 1)
                value, place, packed = held[m, p, own]
                offset = (dither_v if own else near_dither)[part, pl.ds(16 * m + p, UNIT, stride=2), :]
                whole = jnp.floor(packed)
                bound = whole + offset.astype(jnp.float32) * (packed - whole)
                up = (value - high_all[part, at, :] * bound) > low_all[part, at, :] * bound
                held[m, p, own] = take(point_table, jnp.where(up, place + 64, place))

        def store(batch):
            for m, p, own in batch:
                if own:
                    codes[part, pl.ds(16 * m + p, UNIT, stride=2), :] = held.pop((m, p, True)) + held.pop(
                        (m, p, False)
                    )

        for i in range(len(batches) + 2):
            if i < len(batches):
                find_cells(batches[i])
            if 0 <= i - 1 < len(batches):
                round_cells(batches[i - 1])
            if i >= 2:
                store(batches[i - 2])

    def quantize(wave, gap_table, point_table):
        for copy in near_copies[wave]:
            copy.wait_recv()
        parts = WAVES[wave]

        def body(i, carry):
            quantize_chunk(parts[0] + i * (parts[1] - parts[0]), gap_table, point_table)
            return carry

        lax.fori_loop(0, len(parts), body, 0)

    ring = {}

    def order_of(part):
        return ORDERS[part // 3]

    def quarters(order):
        return [lax.rem(here.at[order[0]] + d, RING) * QUARTER for d in range(RING)]

    def scatter_first(part):
        order = order_of(part)
        at = quarters(order)
        right, left = here.near((order[0], 1)), here.near((order[0], 3))

        def move(start, name, skip, to):
            return copies.start(
                codes.at[part, rows_of(start, 8)], landing.at[part, rows_of(LANDING[name] + skip, 8)], to
            )

        ring[part] = [
            move(at[2], "tl", 0, right),
            move(at[2] + 8, "th", 0, left),
            move(at[1] + 8, "fa", 8, right),
            move(at[3], "fb", 0, left),
        ]

    def scatter_second(part):
        order = order_of(part)
        at = quarters(order)
        right, left = here.near((order[0], 1)), here.near((order[0], 3))
        waits = ring[part]
        waits[0].wait_recv()
        add_into(codes, part, at[1], landing, [LANDING["tl"]], 8)
        waits.append(
            copies.start(codes.at[part, rows_of(at[1], 8)], landing.at[part, rows_of(LANDING["fa"], 8)], right)
        )
        waits[1].wait_recv()
        add_into(codes, part, at[3] + 8, landing, [LANDING["th"]], 8)
        waits.append(
            copies.start(
                codes.at[part, rows_of(at[3] + 8, 8)], landing.at[part, rows_of(LANDING["fb"] + 8, 8)], left
            )
        )

    plane = {}

    def piece_at(order, i, j):
        spot = lax.rem(here.at[order[1]] + i, RING) * RING + lax.rem(here.at[order[2]] + j, RING)
        return here.at[order[0]] * QUARTER + spot

    def scatter_plane(part):
        order = order_of(part)
        for copy in ring[part][2:]:
            copy.wait_recv()
        add_into(
            codes, part, here.at[order[0]] * QUARTER, landing, [LANDING["fa"], LANDING["fb"]], QUARTER
        )
        plane[part] = [
            copies.start(
                codes.at[part, rows_of(piece_at(order, i, j), 1)],
                landing.at[part, rows_of(LANDING["plane"] + i * RING + j, 1)],
                here.near((order[1], i), (order[2], j)),
            )
            for i, j in PLANE
        ]

    def scatter_last(part):
        for copy in plane[part]:
            copy.wait_recv()
        firsts = [LANDING["plane"] + i * RING + j for i, j in PLANE]
        add_into(codes, part, piece_at(order_of(part), 0, 0), landing, firsts, 1)

    small_loads[0].wait()
    rotate(0)
    pl.semaphore_wait(barrier, len(partners))
    peak_send(0, 0)
    small_loads[3].start()
    near_dither_copy = copies.start(dither_hbm.at[pl.ds(theirs, PARTS)], near_dither, sibling)
    share(0)
    rotate(1)
    peak_send(1, 0)
    share(1)
    rotate(2)
    peak_send(2, 0)
    share(2)
    for load in small_loads[1:]:
        load.wait()
    gap_table, point_table = tables()
    for turn in (0, 1):
        for wave in range(3):
            peak_take(wave, turn)
            peak_send(wave, turn + 1)
    near_dither_copy.wait_recv()
    for wave in range(3):
        peak_take(wave, 2)
        spread(wave)
        quantize(wave, gap_table, point_table)
        for part in WAVES[wave]:
            scatter_first(part)
    for part in WAVES[0] + WAVES[1]:
        scatter_second(part)
    for part in WAVES[0]:
        scatter_plane(part)
    for part in WAVES[2]:
        scatter_second(part)
    for part in WAVES[1] + WAVES[2]:
        scatter_plane(part)
    for part in range(PARTS):
        scatter_last(part)

    for part in range(PARTS):
        owned[pl.ds(part * UNIT, UNIT), :] = codes[part, rows_of(piece_at(order_of(part), 0, 0), 1), :]
    count = PARTS * UNIT // 2
    both = jnp.concatenate(
        [owned[pl.ds(0, count, stride=2), :], owned[pl.ds(1, count, stride=2), :]], axis=1
    )
    back = jnp.dot(both, had, precision=lax.Precision.HIGHEST, preferred_element_type=jnp.float32)
    owned[pl.ds(0, count, stride=2), :] = back[:, :LANES]
    owned[pl.ds(1, count, stride=2), :] = back[:, LANES:]
    for wave, parts in enumerate(WAVES):
        for i, part in enumerate(parts):
            spot = piece_at(order_of(part), 0, 0)
            word_row = (mine + part) * (CHUNK // 32) + lax.div(spot, 4)
            wide = jnp.broadcast_to(words[pl.ds(word_row, 1), :], (UNIT, LANES))
            word = take(wide, word_lane + 32 * lax.rem(spot, 4))
            row = core * 8 + 2 * i + lax.div(spot, 32)
            wide = jnp.broadcast_to(peaks[wave][pl.ds(row, 1), :], (UNIT, LANES))
            factor = take(wide, 4 * lax.rem(spot, 32) + (sub >> 1)) * (1.0 / 2.0**29)
            grad = owned[pl.ds(part * UNIT, UNIT), :] * factor
            out[mine + part, rows_of(spot, 1), :] = jnp.where((word << word_shift) < 0, -grad, grad)

    last = []
    gather = {}
    arrive = {}

    def send(turn, start, size, to):
        first, count = MEMBERS[turn]
        at = out.at[pl.ds(mine + first, count), rows_of(start, size)]
        return copies.start(at, at, to)

    def gather_plane(turn, i):
        order = ORDERS[turn]
        for j in (2, 1, 3, 0):
            if i + j:
                arrive.setdefault((turn, (RING - i) % RING), []).append(
                    send(turn, piece_at(order, 0, 0), 1, here.near((order[1], i), (order[2], j)))
                )

    def group_of(turn, i):
        order = ORDERS[turn]
        skip = lax.rem(here.at[order[1]] + i, RING) * RING
        starts = [start + skip for start in quarters(order)]
        return starts, here.near((order[0], 1)), here.near((order[0], 3))

    def gather_first(turn, i):
        for copy in arrive[turn, i]:
            copy.wait_recv()
        at, right, left = group_of(turn, i)
        gather[turn, i] = [
            send(turn, at[0], 2, right),
            send(turn, at[0] + 2, 2, left),
            send(turn, at[0] + 2, 2, right),
            send(turn, at[0], 2, left),
        ]
        last.append(send(turn, at[0], RING, sibling))

    def gather_second(turn, i):
        at, right, left = group_of(turn, i)
        waits = gather[turn, i]
        waits[0].wait_recv()
        waits.append(send(turn, at[3], 2, right))
        waits[1].wait_recv()
        waits.append(send(turn, at[1] + 2, 2, left))
        waits[2].wait_recv()
        waits[3].wait_recv()
        last.append(send(turn, at[3], RING, sibling))
        last.append(send(turn, at[1], RING, sibling))

    def gather_last(turn, i):
        at, _, _ = group_of(turn, i)
        for copy in gather[turn, i][4:]:
            copy.wait_recv()
        last.append(send(turn, at[2], RING, sibling))

    for i in GROUPS:
        for turn in range(3):
            gather_plane(turn, i)
    for step in range(len(GROUPS) + 2):
        if step < len(GROUPS):
            for turn in range(3):
                gather_first(turn, GROUPS[step])
        if 0 <= step - 1 < len(GROUPS):
            for turn in range(3):
                gather_second(turn, GROUPS[step - 1])
        if step >= 2:
            for turn in range(3):
                gather_last(turn, GROUPS[step - 2])
    for copy in last:
        copy.wait_recv()
    for copy in copies.late:
        copy.wait_send()


def mean_gradient(gradients, dither, sign_words, level_values, level_points):
    chunks = 2 * PARTS
    whole = pltpu.VMEM((chunks, CHUNK // 2, LANES), jnp.float32)
    quarter = pltpu.VMEM((PARTS, CHUNK // 2, LANES), jnp.float32)
    peak = pltpu.VMEM((16, LANES), jnp.float32)
    anywhere = pl.BlockSpec(memory_space=pltpu.HBM)
    return pl.pallas_call(
        reduce_kernel,
        out_shape=jax.ShapeDtypeStruct((chunks, CHUNK, LANES), jnp.float32),
        in_specs=[anywhere] * 5,
        out_specs=pl.BlockSpec(memory_space=pltpu.VMEM),
        scratch_shapes=[
            pltpu.VMEM((1, ROWS * LANES), jnp.bfloat16),
            pltpu.VMEM((PARTS, CHUNK, LANES), jnp.int32),
            pltpu.VMEM((ROWS // 32, LANES), jnp.int32),
            pltpu.SMEM((16,), jnp.int32),
            pltpu.SMEM((16,), jnp.float32),
            pltpu.VMEM((2, CHUNK, LANES), jnp.float32),
            whole,
            whole,
            pltpu.VMEM((PARTS, CHUNK, LANES), jnp.float32),
            peak,
            peak,
            peak,
            pltpu.VMEM((3, PEAK_COPIES, 16, LANES), jnp.float32),
            quarter,
            quarter,
            quarter,
            quarter,
            quarter,
            pltpu.VMEM((PARTS, CHUNK, LANES), jnp.int32),
            pltpu.VMEM((PARTS, LANDING_UNITS * UNIT, LANES), jnp.float32),
            pltpu.VMEM((PARTS * UNIT, LANES), jnp.float32),
            pltpu.SemaphoreType.DMA((COPIES,)),
            pltpu.SemaphoreType.DMA((COPIES,)),
            pltpu.SemaphoreType.DMA((chunks,)),
            pltpu.SemaphoreType.DMA((4,)),
        ],
        compiler_params=pltpu.CompilerParams(
            collective_id=0, has_side_effects=True, vmem_limit_bytes=47 * 2**20
        ),
        cost_estimate=pl.CostEstimate(flops=2**31, bytes_accessed=12 * 2**20, transcendentals=0),
    )(
        gradients,
        dither.reshape(chunks, CHUNK, LANES),
        sign_words.reshape(-1, LANES),
        level_values,
        level_points,
    )


def body(
    gradients, dither, sign_words, level_values, level_points, params, first_moment, second_moment
):
    mean_grad = mean_gradient(gradients, dither, sign_words, level_values, level_points).reshape(-1)
    new_first = beta_first * first_moment + (1.0 - beta_first) * mean_grad
    new_second = beta_second * second_moment + (1.0 - beta_second) * mean_grad * mean_grad
    update = new_first * (1.0 / bias_first) / (jnp.sqrt(new_second * (1.0 / bias_second)) + epsilon)
    new_params = params - step_rate * update
    return (new_params, new_first, new_second, update)


def solution(mesh):
    placed = (P(("dp", "outer"), None), P(("dp", "outer"), None), P(), P(), P(), P(), P(), P())
    return jax.shard_map(
        body, mesh=mesh, in_specs=placed, out_specs=(P(), P(), P(), P()), check_vma=False
    )
```

```python
import jax
import jax.numpy as jnp
from jax import lax
from jax.experimental import pallas as pl
from jax.experimental.pallas import tpu as pltpu
from jax.sharding import PartitionSpec as P

MESH = pl.DeviceIdType.MESH
LANES = 128
UNIT = 8
ROWS = 8192
CHUNK = 512
RING = 4
PARTS = 8
ORDERS = (("x", "y", "z"), ("y", "z", "x"), ("z", "x", "y"))
MEMBERS = ((0, 3), (3, 3), (6, 2))
WAVES = ((0, 3, 6), (1, 4, 7), (2, 5))
QUARTER = 16
GROUPS = (0, 1, 3, 2)
PLANE = tuple((i, j) for i in (2, 1, 3, 0) for j in (2, 1, 3, 0) if i + j)
BATCH = 16

beta_first = 0.9
beta_second = 0.95
bias_first = 1.0 - 0.9**50
bias_second = 1.0 - 0.95**50
epsilon = 1e-08
step_rate = 0.01


def rows_of(start, count):
    return pl.ds(pl.multiple_of(start * UNIT, UNIT), count * UNIT)


def take(table, idx):
    return jnp.take_along_axis(table, idx, axis=1, mode="promise_in_bounds")


def hadamard_128(length):
    common = lax.broadcasted_iota(jnp.int32, (length, length), 0) & lax.broadcasted_iota(
        jnp.int32, (length, length), 1
    )
    for shift in (4, 2, 1):
        common = common ^ (common >> shift)
    return jnp.where((common & 1) == 1, -128.0, 128.0).astype(jnp.float32)


class Place:
    def __init__(self):
        dp, outer = lax.axis_index("dp"), lax.axis_index("outer")
        self.at = {
            "y": lax.div(dp, 8),
            "x": lax.rem(lax.div(dp, 4), 2) * 2 + lax.div(outer, 2),
            "z": lax.rem(dp, 4),
            "core": lax.rem(outer, 2),
        }

    def near(self, *moves):
        at = dict(self.at)
        for axis, delta in moves:
            at[axis] = lax.rem(at[axis] + delta, 2 if axis == "core" else RING)
        dp = at["y"] * 8 + lax.div(at["x"], 2) * 4 + at["z"]
        return {"dp": dp, "outer": lax.rem(at["x"], 2) * 2 + at["core"]}


class Copies:
    def __init__(self, send, recv):
        self.send, self.recv, self.used, self.late = send, recv, 0, []

    def start(self, src, dst, to, late=True):
        copy = pltpu.make_async_remote_copy(
            src_ref=src,
            dst_ref=dst,
            send_sem=self.send.at[self.used],
            recv_sem=self.recv.at[self.used],
            device_id=to,
            device_id_type=MESH,
        )
        self.used += 1
        if late:
            self.late.append(copy)
        copy.start()
        return copy


PEAK_ROUNDS = (
    tuple((("x", i), ("core", j)) for i in (2, 1, 3, 0) for j in (1, 0) if i + j),
    tuple((("y", i),) for i in (2, 1, 3)),
    tuple((("z", i),) for i in (2, 1, 3)),
)
PEAK_FIRST_SLOT = (0, 7, 10)
PEAK_COPIES = 13
COPIES = 3 * PEAK_COPIES + 1 + PARTS * (2 + 3 + 15) + 3 * (15 + 3 * 10 + 7)


LANDING = {"ring": 0, "plane": 48}
LANDING_UNITS = 64


def add_into(dst, part, start, landing, firsts, count):
    here = rows_of(start, count)
    value = dst[part, here, :]
    for first in firsts:
        value = value + landing[part, rows_of(first, count), :]
    dst[part, here, :] = value


def reduce_kernel(
    grad_hbm, dither_hbm, words_hbm, values_hbm, points_hbm, out,
    grad_v, dither_v, words, level_values, level_points, signed, coef_even, coef_odd, codes,
    peak_a, peak_b, peak_c, peak_in, high_all, low_all, ratio_all,
    near_even, near_odd, near_dither, landing, owned, send_sems, recv_sems, grad_sems, load_sems,
):
    here = Place()
    core = here.at["core"]
    copies = Copies(send_sems, recv_sems)
    peaks = (peak_a, peak_b, peak_c)
    sibling = here.near(("core", 1))
    mine, theirs = core * PARTS, (1 - core) * PARTS

    barrier = pltpu.get_barrier_semaphore()
    partners = [here.near(*moves) for moves in PEAK_ROUNDS[0] + PEAK_ROUNDS[1] + PEAK_ROUNDS[2]]
    for partner in partners:
        pl.semaphore_signal(barrier, inc=1, device_id=partner, device_id_type=MESH)

    small_loads = [
        pltpu.make_async_copy(src, dst, load_sems.at[i])
        for i, (src, dst) in enumerate(
            (
                (words_hbm, words),
                (values_hbm, level_values),
                (points_hbm, level_points),
                (dither_hbm.at[pl.ds(mine, PARTS)], dither_v),
            )
        )
    ]
    small_loads[0].start()
    span = CHUNK * LANES

    def grad_load(part, h):
        chunk = (1 - core + h * (2 * core - 1)) * PARTS + part
        at = pl.ds(pl.multiple_of(chunk * span, span), span)
        return pltpu.make_async_copy(grad_hbm.at[:, at], grad_v.at[:, at], grad_sems.at[part, h])

    for parts in WAVES:
        for h in range(2):
            for part in parts:
                grad_load(part, h).start()
    for load in small_loads[1:3]:
        load.start()

    lane = lax.broadcasted_iota(jnp.int32, (UNIT, LANES), 1)
    sub = lax.broadcasted_iota(jnp.int32, (UNIT, LANES), 0)
    word_lane = sub * 4 + (lane >> 5)
    word_shift = 31 - (lane & 31)
    had = hadamard_128(2 * LANES)
    had_bf = had.astype(jnp.bfloat16)
    for ref in peaks:
        ref[...] = jnp.zeros_like(ref)

    def sign_chunk(chunk, slot):
        for r in range(CHUNK // 32):
            word_row = chunk * (CHUNK // 32) + r
            wide = jnp.broadcast_to(words[pl.ds(word_row, 1), :], (UNIT, LANES))
            for k in range(4):
                word = take(wide, word_lane + 32 * k)
                first = pl.multiple_of(word_row * 4096 + k * 1024, 1024)
                grad = grad_v[:, pl.ds(first, 1024)].astype(jnp.float32).reshape(UNIT, LANES)
                signed[slot, rows_of(r * 4 + k, 1), :] = jnp.where((word << word_shift) < 0, -grad, grad)

    def rotate_chunk(wave, half_core, i, chunk, slot):
        even = signed[slot, pl.ds(0, CHUNK // 2, stride=2), :]
        odd = signed[slot, pl.ds(1, CHUNK // 2, stride=2), :]
        both = jnp.concatenate([even, odd], axis=1).astype(jnp.bfloat16)
        coeffs = jnp.dot(both, had_bf, preferred_element_type=jnp.float32)
        coef_even[chunk] = coeffs[:, :LANES]
        coef_odd[chunk] = coeffs[:, LANES:]
        turned = lax.dot_general(
            had_bf, both, (((1,), (1,)), ((), ())), preferred_element_type=jnp.float32
        )
        top = jnp.max(jnp.abs(turned), axis=0, keepdims=True)
        for j in range(2):
            peaks[wave][pl.ds(half_core * 8 + (2 * i + j), 1), :] = top[:, j * LANES : (j + 1) * LANES]

    def rotate(wave):
        parts = WAVES[wave]

        def body(h, carry):
            half_core = (1 - core) + h * (2 * core - 1)
            for i in range(len(parts) + 1):
                if i < len(parts):
                    grad_load(parts[i], h).wait()
                    sign_chunk(half_core * PARTS + parts[i], i % 2)
                if i >= 1:
                    rotate_chunk(wave, half_core, i - 1, half_core * PARTS + parts[i - 1], (i - 1) % 2)
            return carry

        lax.fori_loop(0, 2, body, 0)

    near_copies = {}

    def share(wave):
        near_copies[wave] = []
        for part in WAVES[wave]:
            for src, dst in ((coef_even, near_even), (coef_odd, near_odd)):
                near_copies[wave].append(copies.start(src.at[theirs + part], dst.at[part], sibling))

    sent_peaks = {}

    def peak_send(wave, turn):
        sent_peaks[wave, turn] = [
            copies.start(
                peaks[wave], peak_in.at[wave, PEAK_FIRST_SLOT[turn] + slot], here.near(*moves), late=False
            )
            for slot, moves in enumerate(PEAK_ROUNDS[turn])
        ]

    def peak_take(wave, turn):
        for copy in sent_peaks[wave, turn]:
            copy.wait_recv()
            copy.wait_send()
        best = peaks[wave][...]
        for slot in range(len(PEAK_ROUNDS[turn])):
            best = jnp.maximum(best, peak_in[wave, PEAK_FIRST_SLOT[turn] + slot])
        peaks[wave][...] = best

    eye = lax.broadcasted_iota(jnp.int32, (LANES, LANES), 0) == lax.broadcasted_iota(
        jnp.int32, (LANES, LANES), 1
    )
    ones = jnp.ones((3 * LANES, LANES), jnp.bfloat16)

    def spread(wave):
        top = peaks[wave][rows_of(core, 1), :]
        whole = jnp.floor(top * (1.0 / 256.0))
        ratio = 32.0 / jnp.maximum(top, 1.0)
        near1 = ratio.astype(jnp.bfloat16).astype(jnp.float32)
        near2 = (ratio - near1).astype(jnp.bfloat16).astype(jnp.float32)
        pieces = (whole * 8.0, (top - whole * 256.0) * (1.0 / 32.0), near1, near2, (ratio - near1) - near2)
        for i, part in enumerate(WAVES[wave]):
            for j in range(2):
                row = 2 * i + j
                diag = [
                    jnp.where(eye, jnp.broadcast_to(piece[row : row + 1, :], (LANES, LANES)), 0.0).astype(
                        jnp.bfloat16
                    )
                    for piece in pieces
                ]
                at = pl.ds(j * LANES, LANES)
                high_all[part, at, :] = jnp.dot(diag[0], ones[:LANES], preferred_element_type=jnp.float32)
                low_all[part, at, :] = jnp.dot(diag[1], ones[:LANES], preferred_element_type=jnp.float32)
                ratio_all[part, at, :] = jnp.dot(
                    jnp.concatenate(diag[2:], axis=1), ones, preferred_element_type=jnp.float32
                )

    def tables():
        cell = (lane & 63) - 32
        low = jnp.full((UNIT, LANES), level_values[0], jnp.int32)
        high = jnp.full((UNIT, LANES), level_values[1], jnp.int32)
        low_point = jnp.full((UNIT, LANES), level_points[0], jnp.float32)
        high_point = jnp.full((UNIT, LANES), level_points[1], jnp.float32)
        for j in range(1, 15):
            passed = cell >= level_values[j]
            low = jnp.where(passed, level_values[j], low)
            high = jnp.where(passed, level_values[j + 1], high)
            low_point = jnp.where(passed, level_points[j], low_point)
            high_point = jnp.where(passed, level_points[j + 1], high_point)
        gap = low.astype(jnp.float32) + (high - low).astype(jnp.float32) * (1.0 / 64.0)
        return gap, jnp.where(lane < 64, low_point, high_point)

    def quantize_chunk(part, gap_table, point_table):
        keys = [(m, p, own) for m in range(CHUNK // 16) for p in (0, 1) for own in (True, False)]
        batches = [keys[i : i + BATCH] for i in range(0, len(keys), BATCH)]
        held = {}

        def find_cells(batch):
            for m, p, own in batch:
                at = rows_of(m, 1)
                if own:
                    value = (coef_even, coef_odd)[p][mine + part, at, :]
                else:
                    value = (near_even, near_odd)[p][part, at, :]
                place = jnp.minimum((value * ratio_all[part, at, :] + 32.0).astype(jnp.int32), 63)
                held[m, p, own] = (value, place, take(gap_table, place))

        def round_cells(batch):
            for m, p, own in batch:
                at = rows_of(m, 1)
                value, place, packed = held[m, p, own]
                offset = (dither_v if own else near_dither)[part, pl.ds(16 * m + p, UNIT, stride=2), :]
                whole = jnp.floor(packed)
                bound = whole + offset.astype(jnp.float32) * (packed - whole)
                up = (value - high_all[part, at, :] * bound) > low_all[part, at, :] * bound
                held[m, p, own] = take(point_table, jnp.where(up, place + 64, place))

        def store(batch):
            for m, p, own in batch:
                if own:
                    codes[part, pl.ds(16 * m + p, UNIT, stride=2), :] = held.pop((m, p, True)) + held.pop(
                        (m, p, False)
                    )

        for i in range(len(batches) + 2):
            if i < len(batches):
                find_cells(batches[i])
            if 0 <= i - 1 < len(batches):
                round_cells(batches[i - 1])
            if i >= 2:
                store(batches[i - 2])

    def quantize(wave, gap_table, point_table):
        for copy in near_copies[wave]:
            copy.wait_recv()
        parts = WAVES[wave]

        def body(i, carry):
            quantize_chunk(parts[0] + i * (parts[1] - parts[0]), gap_table, point_table)
            return carry

        lax.fori_loop(0, len(parts), body, 0)

    ring = {}

    def order_of(part):
        return ORDERS[part // 3]

    def quarters(order):
        return [lax.rem(here.at[order[0]] + d, RING) * QUARTER for d in range(RING)]

    def scatter_ring(part):
        order = order_of(part)
        at = quarters(order)
        ring[part] = [
            copies.start(
                codes.at[part, rows_of(at[d], QUARTER)],
                landing.at[part, rows_of(LANDING["ring"] + (d - 1) * QUARTER, QUARTER)],
                here.near((order[0], d)),
            )
            for d in (2, 1, 3)
        ]

    plane = {}

    def piece_at(order, i, j):
        spot = lax.rem(here.at[order[1]] + i, RING) * RING + lax.rem(here.at[order[2]] + j, RING)
        return here.at[order[0]] * QUARTER + spot

    def scatter_plane(part):
        order = order_of(part)
        for copy in ring[part]:
            copy.wait_recv()
        firsts = [LANDING["ring"] + d * QUARTER for d in range(RING - 1)]
        add_into(codes, part, here.at[order[0]] * QUARTER, landing, firsts, QUARTER)
        plane[part] = [
            copies.start(
                codes.at[part, rows_of(piece_at(order, i, j), 1)],
                landing.at[part, rows_of(LANDING["plane"] + i * RING + j, 1)],
                here.near((order[1], i), (order[2], j)),
            )
            for i, j in PLANE
        ]

    def scatter_last(part):
        for copy in plane[part]:
            copy.wait_recv()
        firsts = [LANDING["plane"] + i * RING + j for i, j in PLANE]
        add_into(codes, part, piece_at(order_of(part), 0, 0), landing, firsts, 1)

    small_loads[0].wait()
    rotate(0)
    pl.semaphore_wait(barrier, len(partners))
    peak_send(0, 0)
    small_loads[3].start()
    near_dither_copy = copies.start(dither_hbm.at[pl.ds(theirs, PARTS)], near_dither, sibling)
    share(0)
    rotate(1)
    peak_send(1, 0)
    share(1)
    rotate(2)
    peak_send(2, 0)
    share(2)
    for load in small_loads[1:]:
        load.wait()
    gap_table, point_table = tables()
    for turn in (0, 1):
        for wave in range(3):
            peak_take(wave, turn)
            peak_send(wave, turn + 1)
    near_dither_copy.wait_recv()
    for wave in range(3):
        peak_take(wave, 2)
        spread(wave)
        quantize(wave, gap_table, point_table)
        for part in WAVES[wave]:
            scatter_ring(part)
    for parts in WAVES:
        for part in parts:
            scatter_plane(part)
    for part in range(PARTS):
        scatter_last(part)

    for part in range(PARTS):
        owned[pl.ds(part * UNIT, UNIT), :] = codes[part, rows_of(piece_at(order_of(part), 0, 0), 1), :]
    count = PARTS * UNIT // 2
    both = jnp.concatenate(
        [owned[pl.ds(0, count, stride=2), :], owned[pl.ds(1, count, stride=2), :]], axis=1
    )
    back = jnp.dot(both, had, precision=lax.Precision.HIGHEST, preferred_element_type=jnp.float32)
    owned[pl.ds(0, count, stride=2), :] = back[:, :LANES]
    owned[pl.ds(1, count, stride=2), :] = back[:, LANES:]
    for wave, parts in enumerate(WAVES):
        for i, part in enumerate(parts):
            spot = piece_at(order_of(part), 0, 0)
            word_row = (mine + part) * (CHUNK // 32) + lax.div(spot, 4)
            wide = jnp.broadcast_to(words[pl.ds(word_row, 1), :], (UNIT, LANES))
            word = take(wide, word_lane + 32 * lax.rem(spot, 4))
            row = core * 8 + 2 * i + lax.div(spot, 32)
            wide = jnp.broadcast_to(peaks[wave][pl.ds(row, 1), :], (UNIT, LANES))
            factor = take(wide, 4 * lax.rem(spot, 32) + (sub >> 1)) * (1.0 / 2.0**29)
            grad = owned[pl.ds(part * UNIT, UNIT), :] * factor
            out[mine + part, rows_of(spot, 1), :] = jnp.where((word << word_shift) < 0, -grad, grad)

    last = []
    gather = {}
    arrive = {}

    def send(turn, start, size, to):
        first, count = MEMBERS[turn]
        at = out.at[pl.ds(mine + first, count), rows_of(start, size)]
        return copies.start(at, at, to)

    def gather_plane(turn, i):
        order = ORDERS[turn]
        for j in (2, 1, 3, 0):
            if i + j:
                arrive.setdefault((turn, (RING - i) % RING), []).append(
                    send(turn, piece_at(order, 0, 0), 1, here.near((order[1], i), (order[2], j)))
                )

    def group_of(turn, i):
        order = ORDERS[turn]
        skip = lax.rem(here.at[order[1]] + i, RING) * RING
        starts = [start + skip for start in quarters(order)]
        return starts, here.near((order[0], 1)), here.near((order[0], 3))

    def gather_first(turn, i):
        for copy in arrive[turn, i]:
            copy.wait_recv()
        at, right, left = group_of(turn, i)
        if i == GROUPS[-1]:
            gather[turn, i] = [
                send(turn, at[0], RING, here.near((ORDERS[turn][0], 2))),
                send(turn, at[0], RING, right),
                send(turn, at[0], RING, left),
            ]
        else:
            gather[turn, i] = [
                send(turn, at[0], 2, right),
                send(turn, at[0] + 2, 2, left),
                send(turn, at[0] + 2, 2, right),
                send(turn, at[0], 2, left),
            ]
        last.append(send(turn, at[0], RING, sibling))

    def gather_second(turn, i):
        at, right, left = group_of(turn, i)
        waits = gather[turn, i]
        if i == GROUPS[-1]:
            for copy, d in ((waits[1], 3), (waits[2], 1), (waits[0], 2)):
                copy.wait_recv()
                last.append(send(turn, at[d], RING, sibling))
            return
        waits[0].wait_recv()
        waits.append(send(turn, at[3], 2, right))
        waits[1].wait_recv()
        waits.append(send(turn, at[1] + 2, 2, left))
        waits[2].wait_recv()
        waits[3].wait_recv()
        last.append(send(turn, at[3], RING, sibling))
        last.append(send(turn, at[1], RING, sibling))

    def gather_last(turn, i):
        at, _, _ = group_of(turn, i)
        for copy in gather[turn, i][4:]:
            copy.wait_recv()
        last.append(send(turn, at[2], RING, sibling))

    for i in GROUPS:
        for turn in range(3):
            gather_plane(turn, i)
    for step in (gather_first, gather_second, gather_last):
        for i in GROUPS if step is not gather_last else GROUPS[:-1]:
            for turn in range(3):
                step(turn, i)
    for copy in last:
        copy.wait_recv()
    for copy in copies.late:
        copy.wait_send()


def mean_gradient(gradients, dither, sign_words, level_values, level_points):
    chunks = 2 * PARTS
    whole = pltpu.VMEM((chunks, CHUNK // 2, LANES), jnp.float32)
    quarter = pltpu.VMEM((PARTS, CHUNK // 2, LANES), jnp.float32)
    peak = pltpu.VMEM((16, LANES), jnp.float32)
    anywhere = pl.BlockSpec(memory_space=pltpu.HBM)
    return pl.pallas_call(
        reduce_kernel,
        out_shape=jax.ShapeDtypeStruct((chunks, CHUNK, LANES), jnp.float32),
        in_specs=[anywhere] * 5,
        out_specs=pl.BlockSpec(memory_space=pltpu.VMEM),
        scratch_shapes=[
            pltpu.VMEM((1, ROWS * LANES), jnp.bfloat16),
            pltpu.VMEM((PARTS, CHUNK, LANES), jnp.int32),
            pltpu.VMEM((ROWS // 32, LANES), jnp.int32),
            pltpu.SMEM((16,), jnp.int32),
            pltpu.SMEM((16,), jnp.float32),
            pltpu.VMEM((2, CHUNK, LANES), jnp.float32),
            whole,
            whole,
            pltpu.VMEM((PARTS, CHUNK, LANES), jnp.float32),
            peak,
            peak,
            peak,
            pltpu.VMEM((3, PEAK_COPIES, 16, LANES), jnp.float32),
            quarter,
            quarter,
            quarter,
            quarter,
            quarter,
            pltpu.VMEM((PARTS, CHUNK, LANES), jnp.int32),
            pltpu.VMEM((PARTS, LANDING_UNITS * UNIT, LANES), jnp.float32),
            pltpu.VMEM((PARTS * UNIT, LANES), jnp.float32),
            pltpu.SemaphoreType.DMA((COPIES,)),
            pltpu.SemaphoreType.DMA((COPIES,)),
            pltpu.SemaphoreType.DMA((PARTS, 2)),
            pltpu.SemaphoreType.DMA((4,)),
        ],
        compiler_params=pltpu.CompilerParams(
            collective_id=0, has_side_effects=True, vmem_limit_bytes=47 * 2**20
        ),
        cost_estimate=pl.CostEstimate(flops=2**31, bytes_accessed=12 * 2**20, transcendentals=0),
    )(
        gradients,
        dither.reshape(chunks, CHUNK, LANES),
        sign_words.reshape(-1, LANES),
        level_values,
        level_points,
    )


def body(
    gradients, dither, sign_words, level_values, level_points, params, first_moment, second_moment
):
    mean_grad = mean_gradient(gradients, dither, sign_words, level_values, level_points).reshape(-1)
    new_first = beta_first * first_moment + (1.0 - beta_first) * mean_grad
    new_second = beta_second * second_moment + (1.0 - beta_second) * mean_grad * mean_grad
    update = new_first * (1.0 / bias_first) / (jnp.sqrt(new_second * (1.0 / bias_second)) + epsilon)
    new_params = params - step_rate * update
    return (new_params, new_first, new_second, update)


def solution(mesh):
    placed = (P(("dp", "outer"), None), P(("dp", "outer"), None), P(), P(), P(), P(), P(), P())
    return jax.shard_map(
        body, mesh=mesh, in_specs=placed, out_specs=(P(), P(), P(), P()), check_vma=False
    )
```

```python
import jax
import jax.numpy as jnp
from jax import lax
from jax.experimental import pallas as pl
from jax.experimental.pallas import tpu as pltpu
from jax.sharding import PartitionSpec as P

MESH = pl.DeviceIdType.MESH
LANES = 128
UNIT = 8
ROWS = 8192
CHUNK = 512
RING = 4
PARTS = 8
ORDERS = (("x", "y", "z"), ("y", "z", "x"), ("z", "x", "y"))
MEMBERS = ((0, 3), (3, 3), (6, 2))
WAVES = ((0, 3, 6), (1, 4, 7), (2, 5))
QUARTER = 16
GROUPS = (0, 1, 3, 2)
PLANE = tuple((i, j) for i in (2, 1, 3, 0) for j in (2, 1, 3, 0) if i + j)
BATCH = 16

beta_first = 0.9
beta_second = 0.95
bias_first = 1.0 - 0.9**50
bias_second = 1.0 - 0.95**50
epsilon = 1e-08
step_rate = 0.01


def rows_of(start, count):
    return pl.ds(pl.multiple_of(start * UNIT, UNIT), count * UNIT)


def take(table, idx):
    return jnp.take_along_axis(table, idx, axis=1, mode="promise_in_bounds")


def hadamard_128(length):
    common = lax.broadcasted_iota(jnp.int32, (length, length), 0) & lax.broadcasted_iota(
        jnp.int32, (length, length), 1
    )
    for shift in (4, 2, 1):
        common = common ^ (common >> shift)
    return jnp.where((common & 1) == 1, -128.0, 128.0).astype(jnp.float32)


class Place:
    def __init__(self):
        dp, outer = lax.axis_index("dp"), lax.axis_index("outer")
        self.at = {
            "y": lax.div(dp, 8),
            "x": lax.rem(lax.div(dp, 4), 2) * 2 + lax.div(outer, 2),
            "z": lax.rem(dp, 4),
            "core": lax.rem(outer, 2),
        }

    def near(self, *moves):
        at = dict(self.at)
        for axis, delta in moves:
            at[axis] = lax.rem(at[axis] + delta, 2 if axis == "core" else RING)
        dp = at["y"] * 8 + lax.div(at["x"], 2) * 4 + at["z"]
        return {"dp": dp, "outer": lax.rem(at["x"], 2) * 2 + at["core"]}


class Copies:
    def __init__(self, send, recv):
        self.send, self.recv, self.used, self.late = send, recv, 0, []

    def start(self, src, dst, to, late=True):
        copy = pltpu.make_async_remote_copy(
            src_ref=src,
            dst_ref=dst,
            send_sem=self.send.at[self.used],
            recv_sem=self.recv.at[self.used],
            device_id=to,
            device_id_type=MESH,
        )
        self.used += 1
        if late:
            self.late.append(copy)
        copy.start()
        return copy


PEAK_ROUNDS = (
    tuple((("x", i), ("core", j)) for i in (2, 1, 3, 0) for j in (1, 0) if i + j),
    tuple((("y", i), ("z", j)) for i, j in PLANE),
)
PEAK_FIRST_SLOT = (0, 7)
PEAK_COPIES = 22
COPIES = 3 * PEAK_COPIES + 1 + PARTS * (2 + 3 + 15) + 3 * (15 + 4 * 7)


LANDING = {"ring": 0, "plane": 48}
LANDING_UNITS = 64


def add_into(dst, part, start, landing, firsts, count):
    here = rows_of(start, count)
    value = dst[part, here, :]
    for first in firsts:
        value = value + landing[part, rows_of(first, count), :]
    dst[part, here, :] = value


def reduce_kernel(
    grad_hbm, dither_hbm, words_hbm, values_hbm, points_hbm, out,
    grad_v, dither_v, words, level_values, level_points, signed, coef_even, coef_odd, codes,
    peak_a, peak_b, peak_c, peak_in, high_all, low_all, ratio_all,
    near_even, near_odd, near_dither, landing, owned, send_sems, recv_sems, grad_sems, load_sems,
):
    here = Place()
    core = here.at["core"]
    copies = Copies(send_sems, recv_sems)
    peaks = (peak_a, peak_b, peak_c)
    sibling = here.near(("core", 1))
    mine, theirs = core * PARTS, (1 - core) * PARTS

    barrier = pltpu.get_barrier_semaphore()
    partners = [here.near(*moves) for moves in PEAK_ROUNDS[0] + PEAK_ROUNDS[1]]
    for partner in partners:
        pl.semaphore_signal(barrier, inc=1, device_id=partner, device_id_type=MESH)

    small_loads = [
        pltpu.make_async_copy(src, dst, load_sems.at[i])
        for i, (src, dst) in enumerate(
            (
                (words_hbm, words),
                (values_hbm, level_values),
                (points_hbm, level_points),
                (dither_hbm.at[pl.ds(mine, PARTS)], dither_v),
            )
        )
    ]
    small_loads[0].start()
    span = CHUNK * LANES

    def grad_load(part, h):
        chunk = (1 - core + h * (2 * core - 1)) * PARTS + part
        at = pl.ds(pl.multiple_of(chunk * span, span), span)
        return pltpu.make_async_copy(grad_hbm.at[:, at], grad_v.at[:, at], grad_sems.at[part, h])

    for parts in WAVES:
        for h in range(2):
            for part in parts:
                grad_load(part, h).start()
    for load in small_loads[1:3]:
        load.start()

    lane = lax.broadcasted_iota(jnp.int32, (UNIT, LANES), 1)
    sub = lax.broadcasted_iota(jnp.int32, (UNIT, LANES), 0)
    word_lane = sub * 4 + (lane >> 5)
    word_shift = 31 - (lane & 31)
    had = hadamard_128(2 * LANES)
    had_bf = had.astype(jnp.bfloat16)
    for ref in peaks:
        ref[...] = jnp.zeros_like(ref)

    def sign_chunk(chunk, slot):
        for r in range(CHUNK // 32):
            word_row = chunk * (CHUNK // 32) + r
            wide = jnp.broadcast_to(words[pl.ds(word_row, 1), :], (UNIT, LANES))
            for k in range(4):
                word = take(wide, word_lane + 32 * k)
                first = pl.multiple_of(word_row * 4096 + k * 1024, 1024)
                grad = grad_v[:, pl.ds(first, 1024)].astype(jnp.float32).reshape(UNIT, LANES)
                signed[slot, rows_of(r * 4 + k, 1), :] = jnp.where((word << word_shift) < 0, -grad, grad)

    def rotate_chunk(wave, half_core, i, chunk, slot):
        even = signed[slot, pl.ds(0, CHUNK // 2, stride=2), :]
        odd = signed[slot, pl.ds(1, CHUNK // 2, stride=2), :]
        both = jnp.concatenate([even, odd], axis=1).astype(jnp.bfloat16)
        coeffs = jnp.dot(both, had_bf, preferred_element_type=jnp.float32)
        coef_even[chunk] = coeffs[:, :LANES]
        coef_odd[chunk] = coeffs[:, LANES:]
        turned = lax.dot_general(
            had_bf, both, (((1,), (1,)), ((), ())), preferred_element_type=jnp.float32
        )
        top = jnp.max(jnp.abs(turned), axis=0, keepdims=True)
        for j in range(2):
            peaks[wave][pl.ds(half_core * 8 + (2 * i + j), 1), :] = top[:, j * LANES : (j + 1) * LANES]

    def rotate(wave):
        parts = WAVES[wave]

        def body(h, carry):
            half_core = (1 - core) + h * (2 * core - 1)
            for i in range(len(parts) + 1):
                if i < len(parts):
                    grad_load(parts[i], h).wait()
                    sign_chunk(half_core * PARTS + parts[i], i % 2)
                if i >= 1:
                    rotate_chunk(wave, half_core, i - 1, half_core * PARTS + parts[i - 1], (i - 1) % 2)
            return carry

        lax.fori_loop(0, 2, body, 0)

    near_copies = {}

    def share(wave):
        near_copies[wave] = []
        for part in WAVES[wave]:
            for src, dst in ((coef_even, near_even), (coef_odd, near_odd)):
                near_copies[wave].append(copies.start(src.at[theirs + part], dst.at[part], sibling))

    sent_peaks = {}

    def peak_send(wave, turn):
        sent_peaks[wave, turn] = [
            copies.start(
                peaks[wave], peak_in.at[wave, PEAK_FIRST_SLOT[turn] + slot], here.near(*moves), late=False
            )
            for slot, moves in enumerate(PEAK_ROUNDS[turn])
        ]

    def peak_take(wave, turn):
        for copy in sent_peaks[wave, turn]:
            copy.wait_recv()
            copy.wait_send()
        best = peaks[wave][...]
        for slot in range(len(PEAK_ROUNDS[turn])):
            best = jnp.maximum(best, peak_in[wave, PEAK_FIRST_SLOT[turn] + slot])
        peaks[wave][...] = best

    eye = lax.broadcasted_iota(jnp.int32, (LANES, LANES), 0) == lax.broadcasted_iota(
        jnp.int32, (LANES, LANES), 1
    )
    ones = jnp.ones((3 * LANES, LANES), jnp.bfloat16)

    def spread(wave):
        top = peaks[wave][rows_of(core, 1), :]
        whole = jnp.floor(top * (1.0 / 256.0))
        ratio = 32.0 / jnp.maximum(top, 1.0)
        near1 = ratio.astype(jnp.bfloat16).astype(jnp.float32)
        near2 = (ratio - near1).astype(jnp.bfloat16).astype(jnp.float32)
        pieces = (whole * 8.0, (top - whole * 256.0) * (1.0 / 32.0), near1, near2, (ratio - near1) - near2)
        for i, part in enumerate(WAVES[wave]):
            for j in range(2):
                row = 2 * i + j
                diag = [
                    jnp.where(eye, jnp.broadcast_to(piece[row : row + 1, :], (LANES, LANES)), 0.0).astype(
                        jnp.bfloat16
                    )
                    for piece in pieces
                ]
                at = pl.ds(j * LANES, LANES)
                high_all[part, at, :] = jnp.dot(diag[0], ones[:LANES], preferred_element_type=jnp.float32)
                low_all[part, at, :] = jnp.dot(diag[1], ones[:LANES], preferred_element_type=jnp.float32)
                ratio_all[part, at, :] = jnp.dot(
                    jnp.concatenate(diag[2:], axis=1), ones, preferred_element_type=jnp.float32
                )

    def tables():
        cell = (lane & 63) - 32
        low = jnp.full((UNIT, LANES), level_values[0], jnp.int32)
        high = jnp.full((UNIT, LANES), level_values[1], jnp.int32)
        low_point = jnp.full((UNIT, LANES), level_points[0], jnp.float32)
        high_point = jnp.full((UNIT, LANES), level_points[1], jnp.float32)
        for j in range(1, 15):
            passed = cell >= level_values[j]
            low = jnp.where(passed, level_values[j], low)
            high = jnp.where(passed, level_values[j + 1], high)
            low_point = jnp.where(passed, level_points[j], low_point)
            high_point = jnp.where(passed, level_points[j + 1], high_point)
        gap = low.astype(jnp.float32) + (high - low).astype(jnp.float32) * (1.0 / 64.0)
        return gap, jnp.where(lane < 64, low_point, high_point)

    def quantize_chunk(part, gap_table, point_table):
        keys = [(m, p, own) for m in range(CHUNK // 16) for p in (0, 1) for own in (True, False)]
        batches = [keys[i : i + BATCH] for i in range(0, len(keys), BATCH)]
        held = {}

        def find_cells(batch):
            for m, p, own in batch:
                at = rows_of(m, 1)
                if own:
                    value = (coef_even, coef_odd)[p][mine + part, at, :]
                else:
                    value = (near_even, near_odd)[p][part, at, :]
                place = jnp.minimum((value * ratio_all[part, at, :] + 32.0).astype(jnp.int32), 63)
                held[m, p, own] = (value, place, take(gap_table, place))

        def round_cells(batch):
            for m, p, own in batch:
                at = rows_of(m, 1)
                value, place, packed = held[m, p, own]
                offset = (dither_v if own else near_dither)[part, pl.ds(16 * m + p, UNIT, stride=2), :]
                whole = jnp.floor(packed)
                bound = whole + offset.astype(jnp.float32) * (packed - whole)
                up = (value - high_all[part, at, :] * bound) > low_all[part, at, :] * bound
                held[m, p, own] = take(point_table, jnp.where(up, place + 64, place))

        def store(batch):
            for m, p, own in batch:
                if own:
                    codes[part, pl.ds(16 * m + p, UNIT, stride=2), :] = held.pop((m, p, True)) + held.pop(
                        (m, p, False)
                    )

        for i in range(len(batches) + 2):
            if i < len(batches):
                find_cells(batches[i])
            if 0 <= i - 1 < len(batches):
                round_cells(batches[i - 1])
            if i >= 2:
                store(batches[i - 2])

    def quantize(wave, gap_table, point_table):
        for copy in near_copies[wave]:
            copy.wait_recv()
        parts = WAVES[wave]

        def body(i, carry):
            quantize_chunk(parts[0] + i * (parts[1] - parts[0]), gap_table, point_table)
            return carry

        lax.fori_loop(0, len(parts), body, 0)

    ring = {}

    def order_of(part):
        return ORDERS[part // 3]

    def quarters(order):
        return [lax.rem(here.at[order[0]] + d, RING) * QUARTER for d in range(RING)]

    def scatter_ring(part):
        order = order_of(part)
        at = quarters(order)
        ring[part] = [
            copies.start(
                codes.at[part, rows_of(at[d], QUARTER)],
                landing.at[part, rows_of(LANDING["ring"] + (d - 1) * QUARTER, QUARTER)],
                here.near((order[0], d)),
            )
            for d in (2, 1, 3)
        ]

    plane = {}

    def piece_at(order, i, j):
        spot = lax.rem(here.at[order[1]] + i, RING) * RING + lax.rem(here.at[order[2]] + j, RING)
        return here.at[order[0]] * QUARTER + spot

    def scatter_plane(part):
        order = order_of(part)
        for copy in ring[part]:
            copy.wait_recv()
        firsts = [LANDING["ring"] + d * QUARTER for d in range(RING - 1)]
        add_into(codes, part, here.at[order[0]] * QUARTER, landing, firsts, QUARTER)
        plane[part] = [
            copies.start(
                codes.at[part, rows_of(piece_at(order, i, j), 1)],
                landing.at[part, rows_of(LANDING["plane"] + i * RING + j, 1)],
                here.near((order[1], i), (order[2], j)),
            )
            for i, j in PLANE
        ]

    def scatter_last(part):
        for copy in plane[part]:
            copy.wait_recv()
        firsts = [LANDING["plane"] + i * RING + j for i, j in PLANE]
        add_into(codes, part, piece_at(order_of(part), 0, 0), landing, firsts, 1)

    small_loads[0].wait()
    rotate(0)
    pl.semaphore_wait(barrier, len(partners))
    peak_send(0, 0)
    small_loads[3].start()
    near_dither_copy = copies.start(dither_hbm.at[pl.ds(theirs, PARTS)], near_dither, sibling)
    share(0)
    rotate(1)
    peak_send(1, 0)
    share(1)
    rotate(2)
    peak_send(2, 0)
    share(2)
    for load in small_loads[1:]:
        load.wait()
    gap_table, point_table = tables()
    for wave in range(3):
        peak_take(wave, 0)
        peak_send(wave, 1)
    near_dither_copy.wait_recv()
    for wave in range(3):
        peak_take(wave, 1)
        spread(wave)
        quantize(wave, gap_table, point_table)
        for part in WAVES[wave]:
            scatter_ring(part)
    for parts in WAVES:
        for part in parts:
            scatter_plane(part)
    for part in range(PARTS):
        scatter_last(part)

    for part in range(PARTS):
        owned[pl.ds(part * UNIT, UNIT), :] = codes[part, rows_of(piece_at(order_of(part), 0, 0), 1), :]
    count = PARTS * UNIT // 2
    both = jnp.concatenate(
        [owned[pl.ds(0, count, stride=2), :], owned[pl.ds(1, count, stride=2), :]], axis=1
    )
    back = jnp.dot(both, had, precision=lax.Precision.HIGHEST, preferred_element_type=jnp.float32)
    owned[pl.ds(0, count, stride=2), :] = back[:, :LANES]
    owned[pl.ds(1, count, stride=2), :] = back[:, LANES:]
    for wave, parts in enumerate(WAVES):
        for i, part in enumerate(parts):
            spot = piece_at(order_of(part), 0, 0)
            word_row = (mine + part) * (CHUNK // 32) + lax.div(spot, 4)
            wide = jnp.broadcast_to(words[pl.ds(word_row, 1), :], (UNIT, LANES))
            word = take(wide, word_lane + 32 * lax.rem(spot, 4))
            row = core * 8 + 2 * i + lax.div(spot, 32)
            wide = jnp.broadcast_to(peaks[wave][pl.ds(row, 1), :], (UNIT, LANES))
            factor = take(wide, 4 * lax.rem(spot, 32) + (sub >> 1)) * (1.0 / 2.0**29)
            grad = owned[pl.ds(part * UNIT, UNIT), :] * factor
            out[mine + part, rows_of(spot, 1), :] = jnp.where((word << word_shift) < 0, -grad, grad)

    last = []
    gather = {}
    arrive = {}

    def send(turn, start, size, to):
        first, count = MEMBERS[turn]
        at = out.at[pl.ds(mine + first, count), rows_of(start, size)]
        return copies.start(at, at, to)

    def gather_plane(turn, i):
        order = ORDERS[turn]
        for j in (2, 1, 3, 0):
            if i + j:
                arrive.setdefault((turn, (RING - i) % RING), []).append(
                    send(turn, piece_at(order, 0, 0), 1, here.near((order[1], i), (order[2], j)))
                )

    def group_of(turn, i):
        order = ORDERS[turn]
        skip = lax.rem(here.at[order[1]] + i, RING) * RING
        return [start + skip for start in quarters(order)]

    def gather_first(turn, i):
        for copy in arrive[turn, i]:
            copy.wait_recv()
        at = group_of(turn, i)
        gather[turn, i] = [(d, send(turn, at[0], RING, here.near((ORDERS[turn][0], d)))) for d in (2, 1, 3)]
        last.append(send(turn, at[0], RING, sibling))

    def gather_second(turn, i):
        at = group_of(turn, i)
        for d, copy in gather[turn, i][1:] + gather[turn, i][:1]:
            copy.wait_recv()
            last.append(send(turn, at[RING - d], RING, sibling))

    for i in GROUPS:
        for turn in range(3):
            gather_plane(turn, i)
    for step in (gather_first, gather_second):
        for i in GROUPS:
            for turn in range(3):
                step(turn, i)
    for copy in last:
        copy.wait_recv()
    for copy in copies.late:
        copy.wait_send()


def mean_gradient(gradients, dither, sign_words, level_values, level_points):
    chunks = 2 * PARTS
    whole = pltpu.VMEM((chunks, CHUNK // 2, LANES), jnp.float32)
    quarter = pltpu.VMEM((PARTS, CHUNK // 2, LANES), jnp.float32)
    peak = pltpu.VMEM((16, LANES), jnp.float32)
    anywhere = pl.BlockSpec(memory_space=pltpu.HBM)
    return pl.pallas_call(
        reduce_kernel,
        out_shape=jax.ShapeDtypeStruct((chunks, CHUNK, LANES), jnp.float32),
        in_specs=[anywhere] * 5,
        out_specs=pl.BlockSpec(memory_space=pltpu.VMEM),
        scratch_shapes=[
            pltpu.VMEM((1, ROWS * LANES), jnp.bfloat16),
            pltpu.VMEM((PARTS, CHUNK, LANES), jnp.int32),
            pltpu.VMEM((ROWS // 32, LANES), jnp.int32),
            pltpu.SMEM((16,), jnp.int32),
            pltpu.SMEM((16,), jnp.float32),
            pltpu.VMEM((2, CHUNK, LANES), jnp.float32),
            whole,
            whole,
            pltpu.VMEM((PARTS, CHUNK, LANES), jnp.float32),
            peak,
            peak,
            peak,
            pltpu.VMEM((3, PEAK_COPIES, 16, LANES), jnp.float32),
            quarter,
            quarter,
            quarter,
            quarter,
            quarter,
            pltpu.VMEM((PARTS, CHUNK, LANES), jnp.int32),
            pltpu.VMEM((PARTS, LANDING_UNITS * UNIT, LANES), jnp.float32),
            pltpu.VMEM((PARTS * UNIT, LANES), jnp.float32),
            pltpu.SemaphoreType.DMA((COPIES,)),
            pltpu.SemaphoreType.DMA((COPIES,)),
            pltpu.SemaphoreType.DMA((PARTS, 2)),
            pltpu.SemaphoreType.DMA((4,)),
        ],
        compiler_params=pltpu.CompilerParams(
            collective_id=0, has_side_effects=True, vmem_limit_bytes=47 * 2**20
        ),
        cost_estimate=pl.CostEstimate(flops=2**31, bytes_accessed=12 * 2**20, transcendentals=0),
    )(
        gradients,
        dither.reshape(chunks, CHUNK, LANES),
        sign_words.reshape(-1, LANES),
        level_values,
        level_points,
    )


def body(
    gradients, dither, sign_words, level_values, level_points, params, first_moment, second_moment
):
    mean_grad = mean_gradient(gradients, dither, sign_words, level_values, level_points).reshape(-1)
    new_first = beta_first * first_moment + (1.0 - beta_first) * mean_grad
    new_second = beta_second * second_moment + (1.0 - beta_second) * mean_grad * mean_grad
    update = new_first * (1.0 / bias_first) / (jnp.sqrt(new_second * (1.0 / bias_second)) + epsilon)
    new_params = params - step_rate * update
    return (new_params, new_first, new_second, update)


def solution(mesh):
    placed = (P(("dp", "outer"), None), P(("dp", "outer"), None), P(), P(), P(), P(), P(), P())
    return jax.shard_map(
        body, mesh=mesh, in_specs=placed, out_specs=(P(), P(), P(), P()), check_vma=False
    )
```

```python
import jax
import jax.numpy as jnp
from jax import lax
from jax.experimental import pallas as pl
from jax.experimental.pallas import tpu as pltpu
from jax.sharding import PartitionSpec as P

MESH = pl.DeviceIdType.MESH
LANES = 128
UNIT = 8
ROWS = 8192
CHUNK = 512
RING = 4
PARTS = 8
ORDERS = (("x", "y", "z"), ("y", "z", "x"), ("z", "x", "y"))
MEMBERS = ((0, 3), (3, 3), (6, 2))
WAVES = ((0, 3, 6), (1, 4, 7), (2, 5))
QUARTER = 16
GROUPS = (0, 1, 3, 2)
PLANE = tuple((i, j) for i in (2, 1, 3, 0) for j in (2, 1, 3, 0) if i + j)
BATCH = 16

beta_first = 0.9
beta_second = 0.95
bias_first = 1.0 - 0.9**50
bias_second = 1.0 - 0.95**50
epsilon = 1e-08
step_rate = 0.01


def rows_of(start, count):
    return pl.ds(pl.multiple_of(start * UNIT, UNIT), count * UNIT)


def take(table, idx):
    return jnp.take_along_axis(table, idx, axis=1, mode="promise_in_bounds")


def hadamard_128(length):
    common = lax.broadcasted_iota(jnp.int32, (length, length), 0) & lax.broadcasted_iota(
        jnp.int32, (length, length), 1
    )
    for shift in (4, 2, 1):
        common = common ^ (common >> shift)
    return jnp.where((common & 1) == 1, -128.0, 128.0).astype(jnp.float32)


class Place:
    def __init__(self):
        dp, outer = lax.axis_index("dp"), lax.axis_index("outer")
        self.at = {
            "y": lax.div(dp, 8),
            "x": lax.rem(lax.div(dp, 4), 2) * 2 + lax.div(outer, 2),
            "z": lax.rem(dp, 4),
            "core": lax.rem(outer, 2),
        }

    def near(self, *moves):
        at = dict(self.at)
        for axis, delta in moves:
            at[axis] = lax.rem(at[axis] + delta, 2 if axis == "core" else RING)
        dp = at["y"] * 8 + lax.div(at["x"], 2) * 4 + at["z"]
        return {"dp": dp, "outer": lax.rem(at["x"], 2) * 2 + at["core"]}


class Copies:
    def __init__(self, send, recv):
        self.send, self.recv, self.used, self.late = send, recv, 0, []

    def start(self, src, dst, to, late=True):
        copy = pltpu.make_async_remote_copy(
            src_ref=src,
            dst_ref=dst,
            send_sem=self.send.at[self.used],
            recv_sem=self.recv.at[self.used],
            device_id=to,
            device_id_type=MESH,
        )
        self.used += 1
        if late:
            self.late.append(copy)
        copy.start()
        return copy


PEAK_ROUNDS = (
    tuple((("x", i), ("core", j)) for i in (2, 1, 3, 0) for j in (1, 0) if i + j),
    tuple((("y", i), ("z", j)) for i, j in PLANE),
)
PEAK_FIRST_SLOT = (0, 7)
PEAK_COPIES = 22
COPIES = 3 * PEAK_COPIES + 1 + PARTS * (2 + 3 + 15) + 3 * (15 + 4 * 7)


LANDING = {"ring": 0, "plane": 48}
LANDING_UNITS = 64


def add_into(dst, part, start, landing, firsts, count):
    here = rows_of(start, count)
    value = dst[part, here, :]
    for first in firsts:
        value = value + landing[part, rows_of(first, count), :]
    dst[part, here, :] = value


def reduce_kernel(
    grad_hbm, dither_hbm, words_hbm, values_hbm, points_hbm, out,
    grad_v, dither_v, words, level_values, level_points, signed, coef_even, coef_odd, codes,
    peak_a, peak_b, peak_c, peak_in, high_all, low_all, ratio_all,
    near_even, near_odd, near_dither, landing, owned, send_sems, recv_sems, grad_sems, load_sems, plane_ready,
):
    here = Place()
    core = here.at["core"]
    copies = Copies(send_sems, recv_sems)
    peaks = (peak_a, peak_b, peak_c)
    sibling = here.near(("core", 1))
    mine, theirs = core * PARTS, (1 - core) * PARTS

    barrier = pltpu.get_barrier_semaphore()
    axes = tuple(((axis, i),) for axis in ("y", "z") for i in (2, 1, 3))
    partners = [here.near(*moves) for moves in PEAK_ROUNDS[0] + axes]
    for partner in partners:
        pl.semaphore_signal(barrier, inc=1, device_id=partner, device_id_type=MESH)

    small_loads = [
        pltpu.make_async_copy(src, dst, load_sems.at[i])
        for i, (src, dst) in enumerate(
            (
                (words_hbm, words),
                (values_hbm, level_values),
                (points_hbm, level_points),
                (dither_hbm.at[pl.ds(mine, PARTS)], dither_v),
            )
        )
    ]
    small_loads[0].start()
    span = CHUNK * LANES

    def grad_load(part, h):
        chunk = (1 - core + h * (2 * core - 1)) * PARTS + part
        at = pl.ds(pl.multiple_of(chunk * span, span), span)
        return pltpu.make_async_copy(grad_hbm.at[:, at], grad_v.at[:, at], grad_sems.at[part, h])

    for parts in WAVES:
        for h in range(2):
            for part in parts:
                grad_load(part, h).start()
    for load in small_loads[1:3]:
        load.start()

    lane = lax.broadcasted_iota(jnp.int32, (UNIT, LANES), 1)
    sub = lax.broadcasted_iota(jnp.int32, (UNIT, LANES), 0)
    word_lane = sub * 4 + (lane >> 5)
    word_shift = 31 - (lane & 31)
    had = hadamard_128(2 * LANES)
    had_bf = had.astype(jnp.bfloat16)
    for ref in peaks:
        ref[...] = jnp.zeros_like(ref)

    def sign_chunk(chunk, slot):
        for r in range(CHUNK // 32):
            word_row = chunk * (CHUNK // 32) + r
            wide = jnp.broadcast_to(words[pl.ds(word_row, 1), :], (UNIT, LANES))
            for k in range(4):
                word = take(wide, word_lane + 32 * k)
                first = pl.multiple_of(word_row * 4096 + k * 1024, 1024)
                grad = grad_v[:, pl.ds(first, 1024)].astype(jnp.float32).reshape(UNIT, LANES)
                signed[slot, rows_of(r * 4 + k, 1), :] = jnp.where((word << word_shift) < 0, -grad, grad)

    def rotate_chunk(wave, half_core, i, chunk, slot):
        even = signed[slot, pl.ds(0, CHUNK // 2, stride=2), :]
        odd = signed[slot, pl.ds(1, CHUNK // 2, stride=2), :]
        both = jnp.concatenate([even, odd], axis=1).astype(jnp.bfloat16)
        coeffs = jnp.dot(both, had_bf, preferred_element_type=jnp.float32)
        coef_even[chunk] = coeffs[:, :LANES]
        coef_odd[chunk] = coeffs[:, LANES:]
        turned = lax.dot_general(
            had_bf, both, (((1,), (1,)), ((), ())), preferred_element_type=jnp.float32
        )
        top = jnp.max(jnp.abs(turned), axis=0, keepdims=True)
        for j in range(2):
            peaks[wave][pl.ds(half_core * 8 + (2 * i + j), 1), :] = top[:, j * LANES : (j + 1) * LANES]

    def rotate(wave):
        parts = WAVES[wave]

        steps = [(h, i) for h in range(2) for i in range(len(parts))]
        half_core = (1 - core, core)
        for t in range(len(steps) + 1):
            if t < len(steps):
                h, i = steps[t]
                grad_load(parts[i], h).wait()
                sign_chunk(half_core[h] * PARTS + parts[i], t % 2)
            if t >= 1:
                h, i = steps[t - 1]
                rotate_chunk(wave, half_core[h], i, half_core[h] * PARTS + parts[i], (t - 1) % 2)

    near_copies = {}

    def share(wave):
        near_copies[wave] = []
        for part in WAVES[wave]:
            for src, dst in ((coef_even, near_even), (coef_odd, near_odd)):
                near_copies[wave].append(copies.start(src.at[theirs + part], dst.at[part], sibling))

    sent_peaks = {}

    def peak_send(wave, turn):
        sent_peaks[wave, turn] = [
            copies.start(
                peaks[wave], peak_in.at[wave, PEAK_FIRST_SLOT[turn] + slot], here.near(*moves), late=False
            )
            for slot, moves in enumerate(PEAK_ROUNDS[turn])
        ]

    def peak_take(wave, turn):
        for copy in sent_peaks[wave, turn]:
            copy.wait_recv()
            copy.wait_send()
        best = peaks[wave][...]
        for slot in range(len(PEAK_ROUNDS[turn])):
            best = jnp.maximum(best, peak_in[wave, PEAK_FIRST_SLOT[turn] + slot])
        peaks[wave][...] = best

    eye = lax.broadcasted_iota(jnp.int32, (LANES, LANES), 0) == lax.broadcasted_iota(
        jnp.int32, (LANES, LANES), 1
    )
    ones = jnp.ones((3 * LANES, LANES), jnp.bfloat16)

    def spread(wave):
        top = peaks[wave][rows_of(core, 1), :]
        whole = jnp.floor(top * (1.0 / 256.0))
        ratio = 32.0 / jnp.maximum(top, 1.0)
        near1 = ratio.astype(jnp.bfloat16).astype(jnp.float32)
        near2 = (ratio - near1).astype(jnp.bfloat16).astype(jnp.float32)
        pieces = (whole * 8.0, (top - whole * 256.0) * (1.0 / 32.0), near1, near2, (ratio - near1) - near2)
        for i, part in enumerate(WAVES[wave]):
            for j in range(2):
                row = 2 * i + j
                diag = [
                    jnp.where(eye, jnp.broadcast_to(piece[row : row + 1, :], (LANES, LANES)), 0.0).astype(
                        jnp.bfloat16
                    )
                    for piece in pieces
                ]
                at = pl.ds(j * LANES, LANES)
                high_all[part, at, :] = jnp.dot(diag[0], ones[:LANES], preferred_element_type=jnp.float32)
                low_all[part, at, :] = jnp.dot(diag[1], ones[:LANES], preferred_element_type=jnp.float32)
                ratio_all[part, at, :] = jnp.dot(
                    jnp.concatenate(diag[2:], axis=1), ones, preferred_element_type=jnp.float32
                )

    def tables():
        cell = (lane & 63) - 32
        low = jnp.full((UNIT, LANES), level_values[0], jnp.int32)
        high = jnp.full((UNIT, LANES), level_values[1], jnp.int32)
        low_point = jnp.full((UNIT, LANES), level_points[0], jnp.float32)
        high_point = jnp.full((UNIT, LANES), level_points[1], jnp.float32)
        for j in range(1, 15):
            passed = cell >= level_values[j]
            low = jnp.where(passed, level_values[j], low)
            high = jnp.where(passed, level_values[j + 1], high)
            low_point = jnp.where(passed, level_points[j], low_point)
            high_point = jnp.where(passed, level_points[j + 1], high_point)
        gap = low.astype(jnp.float32) + (high - low).astype(jnp.float32) * (1.0 / 64.0)
        return gap, jnp.where(lane < 64, low_point, high_point)

    def quantize_chunk(part, gap_table, point_table):
        keys = [(m, p, own) for m in range(CHUNK // 16) for p in (0, 1) for own in (True, False)]
        batches = [keys[i : i + BATCH] for i in range(0, len(keys), BATCH)]
        held = {}

        def find_cells(batch):
            for m, p, own in batch:
                at = rows_of(m, 1)
                if own:
                    value = (coef_even, coef_odd)[p][mine + part, at, :]
                else:
                    value = (near_even, near_odd)[p][part, at, :]
                place = jnp.minimum((value * ratio_all[part, at, :] + 32.0).astype(jnp.int32), 63)
                if p:
                    packed = take(gap_table, place)
                else:
                    packed = jnp.full((UNIT, LANES), gaps[0], jnp.float32)
                    for j in range(1, 15):
                        packed = jnp.where(place >= level_cells[j], gaps[j], packed)
                held[m, p, own] = (value, place, packed)

        def round_cells(batch):
            for m, p, own in batch:
                at = rows_of(m, 1)
                value, place, packed = held[m, p, own]
                offset = (dither_v if own else near_dither)[part, pl.ds(16 * m + p, UNIT, stride=2), :]
                whole = jnp.floor(packed)
                bound = whole + offset.astype(jnp.float32) * (packed - whole)
                up = (value - high_all[part, at, :] * bound) > low_all[part, at, :] * bound
                held[m, p, own] = take(point_table, jnp.where(up, place + 64, place))

        def store(batch):
            for m, p, own in batch:
                if own:
                    codes[part, pl.ds(16 * m + p, UNIT, stride=2), :] = held.pop((m, p, True)) + held.pop(
                        (m, p, False)
                    )

        for i in range(len(batches) + 2):
            if i < len(batches):
                find_cells(batches[i])
            if 0 <= i - 1 < len(batches):
                round_cells(batches[i - 1])
            if i >= 2:
                store(batches[i - 2])

    def quantize(wave, gap_table, point_table):
        for copy in near_copies[wave]:
            copy.wait_recv()
        parts = WAVES[wave]

        def body(i, carry):
            quantize_chunk(parts[0] + i * (parts[1] - parts[0]), gap_table, point_table)
            return carry

        lax.fori_loop(0, len(parts), body, 0)

    ring = {}

    def order_of(part):
        return ORDERS[part // 3]

    def quarters(order):
        return [lax.rem(here.at[order[0]] + d, RING) * QUARTER for d in range(RING)]

    def scatter_ring(part):
        order = order_of(part)
        at = quarters(order)
        ring[part] = [
            copies.start(
                codes.at[part, rows_of(at[d], QUARTER)],
                landing.at[part, rows_of(LANDING["ring"] + (d - 1) * QUARTER, QUARTER)],
                here.near((order[0], d)),
            )
            for d in (2, 1, 3)
        ]

    plane = {}

    def piece_at(order, i, j):
        spot = lax.rem(here.at[order[1]] + i, RING) * RING + lax.rem(here.at[order[2]] + j, RING)
        return here.at[order[0]] * QUARTER + spot

    def scatter_plane(part):
        order = order_of(part)
        for copy in ring[part]:
            copy.wait_recv()
        firsts = [LANDING["ring"] + d * QUARTER for d in range(RING - 1)]
        add_into(codes, part, here.at[order[0]] * QUARTER, landing, firsts, QUARTER)
        plane[part] = [
            copies.start(
                codes.at[part, rows_of(piece_at(order, i, j), 1)],
                landing.at[part, rows_of(LANDING["plane"] + i * RING + j, 1)],
                here.near((order[1], i), (order[2], j)),
            )
            for i, j in PLANE
        ]

    def scatter_last(part):
        for copy in plane[part]:
            copy.wait_recv()
        firsts = [LANDING["plane"] + i * RING + j for i, j in PLANE]
        add_into(codes, part, piece_at(order_of(part), 0, 0), landing, firsts, 1)

    small_loads[0].wait()
    rotate(0)
    pl.semaphore_wait(barrier, len(partners))
    for moves in axes[:3]:
        pl.semaphore_signal(plane_ready, inc=1, device_id=here.near(*moves), device_id_type=MESH)
    peak_send(0, 0)
    small_loads[3].start()
    near_dither_copy = copies.start(dither_hbm.at[pl.ds(theirs, PARTS)], near_dither, sibling)
    share(0)
    rotate(1)
    peak_send(1, 0)
    share(1)
    rotate(2)
    peak_send(2, 0)
    share(2)
    for load in small_loads[1:]:
        load.wait()
    gap_table, point_table = tables()
    level_cells = [level_values[j] + 32 for j in range(15)]
    gaps = [
        level_values[j].astype(jnp.float32) + (level_values[j + 1] - level_values[j]).astype(jnp.float32) / 64.0
        for j in range(15)
    ]
    pl.semaphore_wait(plane_ready, 3)
    for wave in range(3):
        peak_take(wave, 0)
        peak_send(wave, 1)
    near_dither_copy.wait_recv()
    for wave in range(3):
        peak_take(wave, 1)
        spread(wave)
        quantize(wave, gap_table, point_table)
        for part in WAVES[wave]:
            scatter_ring(part)
    for parts in WAVES:
        for part in parts:
            scatter_plane(part)
    for part in range(PARTS):
        scatter_last(part)

    for part in range(PARTS):
        owned[pl.ds(part * UNIT, UNIT), :] = codes[part, rows_of(piece_at(order_of(part), 0, 0), 1), :]
    count = PARTS * UNIT // 2
    both = jnp.concatenate(
        [owned[pl.ds(0, count, stride=2), :], owned[pl.ds(1, count, stride=2), :]], axis=1
    )
    back = jnp.dot(both, had, precision=lax.Precision.HIGHEST, preferred_element_type=jnp.float32)
    owned[pl.ds(0, count, stride=2), :] = back[:, :LANES]
    owned[pl.ds(1, count, stride=2), :] = back[:, LANES:]
    for wave, parts in enumerate(WAVES):
        for i, part in enumerate(parts):
            spot = piece_at(order_of(part), 0, 0)
            word_row = (mine + part) * (CHUNK // 32) + lax.div(spot, 4)
            wide = jnp.broadcast_to(words[pl.ds(word_row, 1), :], (UNIT, LANES))
            word = take(wide, word_lane + 32 * lax.rem(spot, 4))
            row = core * 8 + 2 * i + lax.div(spot, 32)
            wide = jnp.broadcast_to(peaks[wave][pl.ds(row, 1), :], (UNIT, LANES))
            factor = take(wide, 4 * lax.rem(spot, 32) + (sub >> 1)) * (1.0 / 2.0**29)
            grad = owned[pl.ds(part * UNIT, UNIT), :] * factor
            out[mine + part, rows_of(spot, 1), :] = jnp.where((word << word_shift) < 0, -grad, grad)

    last = []
    gather = {}
    arrive = {}

    def send(turn, start, size, to):
        first, count = MEMBERS[turn]
        at = out.at[pl.ds(mine + first, count), rows_of(start, size)]
        return copies.start(at, at, to)

    def gather_plane(turn, i):
        order = ORDERS[turn]
        for j in (2, 1, 3, 0):
            if i + j:
                arrive.setdefault((turn, (RING - i) % RING), []).append(
                    send(turn, piece_at(order, 0, 0), 1, here.near((order[1], i), (order[2], j)))
                )

    def group_of(turn, i):
        order = ORDERS[turn]
        skip = lax.rem(here.at[order[1]] + i, RING) * RING
        return [start + skip for start in quarters(order)]

    def gather_first(turn, i):
        for copy in arrive[turn, i]:
            copy.wait_recv()
        at = group_of(turn, i)
        gather[turn, i] = [(d, send(turn, at[0], RING, here.near((ORDERS[turn][0], d)))) for d in (2, 1, 3)]
        last.append(send(turn, at[0], RING, sibling))

    def gather_second(turn, i):
        at = group_of(turn, i)
        for d, copy in gather[turn, i][1:] + gather[turn, i][:1]:
            copy.wait_recv()
            last.append(send(turn, at[RING - d], RING, sibling))

    for i in GROUPS:
        for turn in range(3):
            gather_plane(turn, i)
    for step in (gather_first, gather_second):
        for i in GROUPS:
            for turn in range(3):
                step(turn, i)
    for copy in last:
        copy.wait_recv()
    for copy in copies.late:
        copy.wait_send()


def mean_gradient(gradients, dither, sign_words, level_values, level_points):
    chunks = 2 * PARTS
    whole = pltpu.VMEM((chunks, CHUNK // 2, LANES), jnp.float32)
    quarter = pltpu.VMEM((PARTS, CHUNK // 2, LANES), jnp.float32)
    peak = pltpu.VMEM((16, LANES), jnp.float32)
    anywhere = pl.BlockSpec(memory_space=pltpu.HBM)
    return pl.pallas_call(
        reduce_kernel,
        out_shape=jax.ShapeDtypeStruct((chunks, CHUNK, LANES), jnp.float32),
        in_specs=[anywhere] * 5,
        out_specs=pl.BlockSpec(memory_space=pltpu.VMEM),
        scratch_shapes=[
            pltpu.VMEM((1, ROWS * LANES), jnp.bfloat16),
            pltpu.VMEM((PARTS, CHUNK, LANES), jnp.int32),
            pltpu.VMEM((ROWS // 32, LANES), jnp.int32),
            pltpu.SMEM((16,), jnp.int32),
            pltpu.SMEM((16,), jnp.float32),
            pltpu.VMEM((2, CHUNK, LANES), jnp.float32),
            whole,
            whole,
            pltpu.VMEM((PARTS, CHUNK, LANES), jnp.float32),
            peak,
            peak,
            peak,
            pltpu.VMEM((3, PEAK_COPIES, 16, LANES), jnp.float32),
            quarter,
            quarter,
            quarter,
            quarter,
            quarter,
            pltpu.VMEM((PARTS, CHUNK, LANES), jnp.int32),
            pltpu.VMEM((PARTS, LANDING_UNITS * UNIT, LANES), jnp.float32),
            pltpu.VMEM((PARTS * UNIT, LANES), jnp.float32),
            pltpu.SemaphoreType.DMA((COPIES,)),
            pltpu.SemaphoreType.DMA((COPIES,)),
            pltpu.SemaphoreType.DMA((PARTS, 2)),
            pltpu.SemaphoreType.DMA((4,)),
            pltpu.SemaphoreType.REGULAR,
        ],
        compiler_params=pltpu.CompilerParams(
            collective_id=0, has_side_effects=True, vmem_limit_bytes=47 * 2**20
        ),
        cost_estimate=pl.CostEstimate(flops=2**31, bytes_accessed=12 * 2**20, transcendentals=0),
    )(
        gradients,
        dither.reshape(chunks, CHUNK, LANES),
        sign_words.reshape(-1, LANES),
        level_values,
        level_points,
    )


def body(
    gradients, dither, sign_words, level_values, level_points, params, first_moment, second_moment
):
    mean_grad = mean_gradient(gradients, dither, sign_words, level_values, level_points).reshape(-1)
    new_first = beta_first * first_moment + (1.0 - beta_first) * mean_grad
    new_second = beta_second * second_moment + (1.0 - beta_second) * mean_grad * mean_grad
    update = new_first * (1.0 / bias_first) / (jnp.sqrt(new_second * (1.0 / bias_second)) + epsilon)
    new_params = params - step_rate * update
    return (new_params, new_first, new_second, update)


def solution(mesh):
    placed = (P(("dp", "outer"), None), P(("dp", "outer"), None), P(), P(), P(), P(), P(), P())
    return jax.shard_map(
        body, mesh=mesh, in_specs=placed, out_specs=(P(), P(), P(), P()), check_vma=False
    )
```
